32 devices in a mesh: section: 2 (over x), dp: 16 (over z, y, core).
Axes of the slice: x: 2, y: 2, z: 4, core: 2. Of those that a mesh axis runs over, the one named last changes fastest.
Arguments:
- tokens: bfloat16 [6, 64, 65, 384], P(None, 'dp'), may hold values from -6 to 6
- mask_emb: bfloat16 [384], replicated, may hold values from -5 to 5
- mask_idx: int32 [6, 64, 28], P(None, 'dp'), may hold values from 0 to 63, as said below
- centers: float32 [3, 6, 64, 64], P(None, None, 'dp'), may hold values from -1 to 1
- cotangent: bfloat16 [6, 64, 65, 384], P(None, 'dp'), may hold values from -6 to 6
- ln_gain: float32 [2, 2, 384], P('section'), may hold values from 0.5 to 1.5
- ln_bias: float32 [2, 2, 384], P('section'), may hold values from -1 to 1
- qkv_w: bfloat16 [2, 384, 1152], P('section'), may hold values from -0.3125 to 0.3125
- proj_w: bfloat16 [2, 384, 384], P('section'), may hold values from -0.875 to 0.875
- out_bias: float32 [2, 2, 384], P('section'), may hold values from -1 to 1
- fc1_w: bfloat16 [2, 384, 1536], P('section'), may hold values from -0.3125 to 0.3125
- fc1_b: float32 [2, 1536], P('section'), may hold values from -1 to 1
- fc2_w: bfloat16 [2, 1536, 384], P('section'), may hold values from -0.15625 to 0.15625
- pos_w1: float32 [2, 3, 128], P('section'), may hold values from -4 to 4
- pos_b1: float32 [2, 128], P('section'), may hold values from -2 to 2
- pos_w2: bfloat16 [2, 128, 384], P('section'), may hold values from -0.5 to 0.5
- pos_b2: float32 [2, 384], P('section'), may hold values from -1.5 to 1.5
Outputs:
- section_out: bfloat16 [2, 6, 64, 65, 384], P('section', None, 'dp')
- section_grad: float32 [2, 6, 64, 65, 384], P('section', None, 'dp')
- mask_grad: float32 [384], replicated
- ln_gain_grad: float32 [2, 2, 384], P('section')
- ln_bias_grad: float32 [2, 2, 384], P('section')
- qkv_w_grad: float32 [2, 384, 1152], P('section')
- proj_w_grad: float32 [2, 384, 384], P('section')
- out_bias_grad: float32 [2, 2, 384], P('section')
- fc1_w_grad: float32 [2, 384, 1536], P('section')
- fc1_b_grad: float32 [2, 1536], P('section')
- fc2_w_grad: float32 [2, 1536, 384], P('section')
- pos_w1_grad: float32 [2, 3, 128], P('section')
- pos_b1_grad: float32 [2, 128], P('section')
- pos_w2_grad: float32 [2, 128, 384], P('section')
- pos_b2_grad: float32 [2, 384], P('section')
The draws below stay inside these ranges and needn't reach their ends.
Inputs may be any that keep to these rules, and one draw needn't show every extreme that they name: `mask_idx`: each cloud's row lists one run of consecutive patch numbers, counted modulo 64, of 16 to 28 patches, in order, the last one repeated to fill the row.
All inputs are finite; a program needn't handle non-finite values.
Results may differ from the reference program's by a relative error of at most 0.012.
Values may be sent and summed in bfloat16 or wider, within the bound.
No kernel may reach another device: no remote copies, remote signals or barrier semaphores. Data moves between devices by JAX's collectives and lax.ppermute only.
A program may use at most 192 MiB of HBM per device.

```python
import jax
import jax.numpy as jnp
from jax import lax

D = 384
FF = 1536
HEADS = 6
HD = 64
PH = 128
PATCHES = 64
MASKW = 28
MICRO = 6
CPM = 4
CLOUDS = 64
N_DP = 16


def draw_mask_idx(key, part):
    key = jax.random.fold_in(key, 11)
    start_key, length_key = jax.random.split(key)
    starts = jax.random.randint(start_key, (MICRO, CLOUDS), 0, PATCHES)
    lengths = jax.random.randint(length_key, (MICRO, CLOUDS), PATCHES // 4, MASKW + 1)
    starts = starts.at[0, 0].set(PATCHES * 3 // 4)
    lengths = lengths.at[0, 0].set(MASKW)
    offsets = jnp.minimum(jnp.arange(MASKW), lengths[..., None] - 1)
    return ((starts[..., None] + offsets) % PATCHES).astype(jnp.int32)


def steps_of(rng, extent, pieces, low, largest):
    factor_of = 1.0
    for axis_at, parts in pieces:
        steps = jax.random.uniform(jax.random.fold_in(jax.random.fold_in(rng, 6), axis_at), (parts,), jnp.float32, low / len(pieces), largest / len(pieces))
        factor_of = factor_of * jnp.repeat(jnp.exp(steps), extent[axis_at] // parts).reshape((-1,) + (1,) * (len(extent) - 1 - axis_at))
    return factor_of


def bell_draw(rng, dims, spread, most, pieces=(), kind=jnp.bfloat16):
    result = spread * jax.random.normal(rng, dims, jnp.float32)
    if pieces:
        result = result * steps_of(rng, dims, pieces, -0.22, 0.18)
    return jnp.clip(result, -most, most).astype(kind)


def setup_inputs(seed: int = 0) -> dict:
    streams_of = jax.random.split(jax.random.key(seed), 18)
    tokens = bell_draw(streams_of[0], (MICRO, CLOUDS, PATCHES + 1, D), 1.0, 6.0, ((1, 16),))
    mask_emb = bell_draw(streams_of[1], (D,), 1.0, 5.0)
    mask_idx = draw_mask_idx(jax.random.fold_in(streams_of[17], 71), 0)
    centers = jnp.clip(jax.random.uniform(streams_of[3], (3, MICRO, CLOUDS, PATCHES), jnp.float32, -1.0, 1.0) * steps_of(streams_of[3], (3, MICRO, CLOUDS, PATCHES), ((2, 16),), -0.4, 0.0), -1.0, 1.0)
    cotangent = bell_draw(streams_of[4], (MICRO, CLOUDS, PATCHES + 1, D), 1.0, 6.0, ((1, 16),))
    ln_gain = jnp.clip(1.0 + 0.1 * jax.random.normal(streams_of[5], (2, 2, D), jnp.float32), 0.5, 1.5)
    ln_bias = bell_draw(streams_of[6], (2, 2, D), 0.2, 1.0, ((0, 2),), jnp.float32)
    qkv_w = bell_draw(streams_of[7], (2, D, 3 * D), D ** -0.5, 0.3125, ((0, 2),))
    proj_w = bell_draw(streams_of[8], (2, D, D), (D // 8) ** -0.5, 0.875, ((0, 2),))
    out_bias = bell_draw(streams_of[9], (2, 2, D), 0.2, 1.0, ((0, 2),), jnp.float32)
    fc1_w = bell_draw(streams_of[10], (2, D, FF), D ** -0.5, 0.3125, ((0, 2),))
    fc1_b = bell_draw(streams_of[11], (2, FF), 0.2, 1.0, ((0, 2),), jnp.float32)
    fc2_w = bell_draw(streams_of[12], (2, FF, D), FF ** -0.5, 0.15625, ((0, 2),))
    pos_w1 = bell_draw(streams_of[13], (2, 3, PH), 1.0, 4.0, ((0, 2),), jnp.float32)
    pos_b1 = bell_draw(streams_of[14], (2, PH), 0.5, 2.0, ((0, 2),), jnp.float32)
    pos_w2 = bell_draw(streams_of[15], (2, PH, D), PH ** -0.5, 0.5, ((0, 2),))
    pos_b2 = bell_draw(streams_of[16], (2, D), 0.3, 1.5, ((0, 2),), jnp.float32)
    return {"tokens": tokens, "mask_emb": mask_emb, "mask_idx": mask_idx, "centers": centers, "cotangent": cotangent, "ln_gain": ln_gain, "ln_bias": ln_bias, "qkv_w": qkv_w, "proj_w": proj_w, "out_bias": out_bias, "fc1_w": fc1_w, "fc1_b": fc1_b, "fc2_w": fc2_w, "pos_w1": pos_w1, "pos_b1": pos_b1, "pos_w2": pos_w2, "pos_b2": pos_b2}


EPS = 1e-05
HIGH = lax.Precision.HIGHEST

@jax.custom_vjp
def low(v):
    return lax.optimization_barrier(v.astype(jnp.bfloat16)).astype(jnp.float32)

@jax.custom_vjp
def low_back(v):
    return v

def low_keep(v):
    return (low(v), None)

def low_pass(kept, grad):
    return (grad,)

def back_keep(v):
    return (v, None)

def back_low(kept, grad):
    return (low(grad),)
low.defvjp(low_keep, low_pass)
low_back.defvjp(back_keep, back_low)

def norm_apply(values, norm_gain, norm_bias):
    average = lax.optimization_barrier(jnp.mean(values, axis=-1, keepdims=True))
    centred = values - average
    variance = lax.optimization_barrier(jnp.mean(centred * centred, axis=-1, keepdims=True))
    return centred * lax.rsqrt(variance + EPS) * norm_gain + norm_bias

def gelu_exact(values):
    return jax.nn.gelu(values, approximate=False)

def position_input(centre, pos_w1, pos_b1):
    return centre[0][..., None] * pos_w1[0] + centre[1][..., None] * pos_w1[1] + centre[2][..., None] * pos_w1[2] + pos_b1

def matmul(left, right):
    return jnp.einsum('cpk,kn->cpn', left, right, precision=HIGH)

def block_forward(inputs, centre, ln_gain, ln_bias, qkv_w, proj_w, out_bias, fc1_w, fc1_b, fc2_w, pos_w1, pos_b1, pos_w2, pos_b2):
    cloud_count, row_count, model_width = inputs.shape
    pos_in = position_input(centre, pos_w1, pos_b1)
    pos_hidden = low(gelu_exact(pos_in))
    residual = inputs + (low_back(matmul(pos_hidden, pos_w2)) + pos_b2)
    normed = low(norm_apply(residual, ln_gain[0], ln_bias[0]))
    packed_qkv = low(low_back(matmul(normed, qkv_w)))
    queries = packed_qkv[..., :model_width].reshape(cloud_count, row_count, HEADS, HD)
    key_heads = packed_qkv[..., model_width:2 * model_width].reshape(cloud_count, row_count, HEADS, HD)
    values = packed_qkv[..., 2 * model_width:].reshape(cloud_count, row_count, HEADS, HD)
    scores = low_back(jnp.einsum('cqhd,ckhd->chqk', queries, key_heads, precision=HIGH) * HD ** (-0.5))
    attn_probs = jax.nn.softmax(scores, axis=-1)
    attended = low(low_back(jnp.einsum('chqk,ckhd->cqhd', low(attn_probs), values, precision=HIGH))).reshape(cloud_count, row_count, model_width)
    after_attn = residual + low_back(matmul(attended, proj_w)) + out_bias[0]
    normed_two = low(norm_apply(after_attn, ln_gain[1], ln_bias[1]))
    hidden = low(gelu_exact(low_back(matmul(normed_two, fc1_w)) + fc1_b))
    return after_attn + low_back(matmul(hidden, fc2_w)) + out_bias[1]

def two_layers(tokens_f, memb, masked, centre, delta, weights):
    first_in = jnp.where(masked[..., None] > 0, memb, tokens_f)
    y_first = block_forward(first_in, centre, *[weight[0] for weight in weights])
    y_second = block_forward(low(low_back(y_first)) + delta, centre, *[weight[1] for weight in weights])
    return (y_first, y_second)

def reference(tokens, mask_emb, mask_idx, centers, cotangent, ln_gain, ln_bias, qkv_w, proj_w, out_bias, fc1_w, fc1_b, fc2_w, pos_w1, pos_b1, pos_w2, pos_b2):
    weights = tuple((weight.astype(jnp.float32) for weight in (ln_gain, ln_bias, qkv_w, proj_w, out_bias, fc1_w, fc1_b, fc2_w, pos_w1, pos_b1, pos_w2, pos_b2)))
    block_total = MICRO * N_DP
    row_count = PATCHES + 1
    patch_ids = jnp.arange(PATCHES, dtype=jnp.int32)
    hits = jnp.any(mask_idx[..., :, None] == patch_ids, axis=-2).astype(jnp.int32)
    masked = jnp.concatenate([jnp.zeros((MICRO, CLOUDS, 1), dtype=jnp.int32), hits], axis=-1).reshape(block_total, CPM, row_count)
    tok_blocks = tokens.reshape(block_total, CPM, row_count, D)
    cot_blocks = cotangent.reshape(block_total, CPM, row_count, D)
    centre_all = jnp.concatenate([jnp.zeros((3, MICRO, CLOUDS, 1), jnp.float32), centers], axis=-1)
    centre_blocks = jnp.moveaxis(centre_all.reshape(3, block_total, CPM, row_count), 1, 0)
    memb = mask_emb.astype(jnp.float32)

    def block_step(running, block_item):
        tok_b, cot_b, mask_b, centre_b = block_item
        tok_f = tok_b.astype(jnp.float32)
        delta = jnp.zeros_like(tok_f)

        def run_pair(tok_in, memb_in, delta_in, weight_in):
            return two_layers(tok_in, memb_in, mask_b, centre_b, delta_in, weight_in)
        (y_first, y_second), backward = jax.vjp(run_pair, tok_f, memb, delta, weights)
        d_tok, d_memb, d_delta, d_weights = backward((jnp.zeros_like(y_first), cot_b.astype(jnp.float32)))
        running = (running[0] + d_memb, tuple((total + piece for total, piece in zip(running[1], d_weights))))
        return (running, (y_first.astype(jnp.bfloat16), y_second.astype(jnp.bfloat16), d_tok, d_delta))
    initial = (jnp.zeros((D,), jnp.float32), tuple((jnp.zeros_like(weight) for weight in weights)))
    (mask_grad, grads), (y_firsts, y_seconds, d_toks, d_deltas) = lax.scan(block_step, initial, (tok_blocks, cot_blocks, masked, centre_blocks))
    full_shape = (MICRO, CLOUDS, row_count, D)
    section_out = jnp.stack([y_firsts.reshape(full_shape), y_seconds.reshape(full_shape)])
    section_grad = jnp.stack([d_toks.reshape(full_shape), d_deltas.reshape(full_shape)])
    return (section_out, section_grad, mask_grad, grads[0], grads[1], grads[2], grads[3], grads[4], grads[5], grads[6], grads[7], grads[8], grads[9], grads[10], grads[11])
```

```python
import functools

import jax
import jax.numpy as jnp
from jax import lax
from jax.experimental import pallas as pl
from jax.experimental.pallas import tpu as pltpu
from jax.sharding import PartitionSpec as P

HEADS = 6
HD = 64
EPS = 1e-05
LANES = 128
MIB = 1 << 20
LAG = 2
QKV_COLS = 768
F_COLS = 256
G_COLS = 1536
VMEM_LIMIT = 12 * MIB

F32 = jnp.float32
BF16 = jnp.bfloat16

ERF_P = 0.375
ERF_C = (
    0.21137403,
    0.21522517,
    0.16911028,
    0.27655959,
    -0.12036233,
    0.3812622,
    -0.1331683,
)
ROOT_HALF = 0.7071067811865476
INV_ROOT_TWO_PI = 0.3989422804014327


def gelu_pair(f):
    den = 1.0 + (ERF_P * ROOT_HALF) * jnp.abs(f)
    t = pl.reciprocal(den, approx=True)
    t = t * (2.0 - den * t)
    e = jnp.exp((f * f) * -0.5)
    poly = 0.5 * ERF_C[-1]
    for c in ERF_C[-2::-1]:
        poly = poly * t + 0.5 * c
    q = e * (t * poly)
    cdf = jnp.where(f >= 0, 1.0 - q, q)
    return f * cdf, cdf + f * (INV_ROOT_TWO_PI * e)


def dot(a, b):
    return jnp.dot(a, b, preferred_element_type=F32)


def dot_t(a, b):
    return lax.dot_general(a, b, (((1,), (1,)), ((), ())), preferred_element_type=F32)


def dot_c(a, b):
    return lax.dot_general(a, b, (((0,), (0,)), ((), ())), preferred_element_type=F32)


def dot_c_f32(a, b):
    return lax.dot_general(
        a, b, (((0,), (0,)), ((), ())), preferred_element_type=F32, precision=lax.Precision.HIGHEST
    )


def dot_f32(a, b):
    return jnp.dot(a, b, preferred_element_type=F32, precision=lax.Precision.HIGHEST)


def centre_rows(centers_ref, cloud):
    patch_count = centers_ref.shape[2]
    rows = [centers_ref[i, pl.ds(cloud, 1), :] for i in range(3)]
    body = jnp.concatenate(rows, axis=0)
    body = jnp.concatenate([jnp.zeros((3, 1), F32), body], axis=1)
    body = jnp.concatenate([body, jnp.zeros((3, LANES - 1 - patch_count), F32)], axis=1)
    return jnp.concatenate([body, jnp.ones((1, LANES), F32), jnp.zeros((4, LANES), F32)], axis=0)


def masked_rows(mask_idx_ref, cloud, padded):
    ids = mask_idx_ref[pl.ds(cloud, 1), :]
    rows = lax.broadcasted_iota(jnp.int32, (padded, ids.shape[1]), 0) - 1
    return jnp.max((rows == ids).astype(F32), axis=1, keepdims=True) > 0.0


def norm_stats(v):
    width = v.shape[1]
    mean = jnp.sum(v, axis=1, keepdims=True) * (1.0 / width)
    cen = v - mean
    var = jnp.sum(cen * cen, axis=1, keepdims=True) * (1.0 / width)
    rs = lax.rsqrt(var + EPS)
    return cen * rs, rs


def norm_back(dn, gain, vhat, rs):
    width = dn.shape[1]
    dg = dn * gain
    m1 = jnp.sum(dg, axis=1, keepdims=True) * (1.0 / width)
    m2 = jnp.sum(dg * vhat, axis=1, keepdims=True) * (1.0 / width)
    return rs * (dg - m1 - vhat * m2)


def col_chunks(width, step):
    return [pl.ds(at, min(step, width - at)) for at in range(0, width, step)]


def colsum(v):
    return jnp.sum(v, axis=0, keepdims=True)


def stack_heads(pair, low):
    zero = jnp.zeros_like(pair)
    return jnp.concatenate([jnp.where(low, pair, zero), jnp.where(low, zero, pair)], axis=0)


def merge_heads(stacked, low):
    n = stacked.shape[0] // 2
    return jnp.where(low, stacked[:n], stacked[n:])


SAVES = (
    ("pc", 1, BF16),
    ("gz", 1, BF16),
    ("vh1", 3, BF16),
    ("n1", 3, BF16),
    ("qkv", 9, BF16),
    ("o", 3, BF16),
    ("vh2", 3, BF16),
    ("n2", 3, BF16),
    ("u", 12, BF16),
    ("gu", 12, BF16),
    ("dyb", 3, BF16),
    ("yb", 3, BF16),
)


def alloc_kernel(*refs):
    for ref in refs[-2:]:
        ref[...] = jnp.zeros(ref.shape, ref.dtype)


def tick_kernel(cfg, *refs):
    (M, C, rows_in, PR, D, FF) = cfg
    R = C * PR
    names = ["tick", "role", "tokens", "memb", "mask_idx", "centers", "cot"]
    names += ["gain", "bias", "qkv_w", "proj_w", "ob", "fc1_w", "fc1_b", "fc2_w", "pw1", "pb1", "pw2", "pb2"]
    names += ["recv"]
    buf_names = [s[0] for s in SAVES] + ["p", "rs1", "rs2", "dx", "small"]
    names += ["old_" + b for b in buf_names]
    names += buf_names + ["send"]
    scratch_names = ["X", "H", "Q", "O", "G", "S"]
    names += scratch_names
    r = dict(zip(names, refs, strict=True))
    tick, role = r["tick"][0], r["role"][0]
    first = role == 0
    f_at = jnp.where(first, tick, tick - LAG)
    g_at = jnp.where(first, tick - 2 * LAG, tick - LAG)
    f_on, g_on = ((at >= 0) & (at < M) for at in (f_at, g_at))
    f_chunk, g_chunk = (jnp.clip(at, 0, M - 1) for at in (f_at, g_at))
    pairs = HEADS // 2
    low = lax.broadcasted_iota(jnp.int32, (PR, LANES), 1) < HD
    scale = HD**-0.5
    X, H, Q, O, G, S = (r[s] for s in scratch_names)

    def position(chunk, carry):
        base = pl.multiple_of(chunk * R, 16)
        w1 = jnp.concatenate([r["pw1"][...], r["pb1"][...], jnp.zeros((4, LANES), F32)], axis=0)
        for c in range(C):
            z = dot_c_f32(centre_rows(r["centers"], chunk * C + c), w1)
            O[pl.ds(c * PR, PR), :LANES] = z[:PR]
        pc, gz = gelu_pair(O[:, :LANES])
        r["pc"][pl.ds(base, R), :] = pc.astype(BF16)
        r["gz"][pl.ds(base, R), :] = gz.astype(BF16)
        return carry

    early = -(-M // LAG)
    pos_from = jnp.where(first, f_chunk, jnp.minimum(tick * early, M))
    pos_to = jnp.where(first, pos_from + f_on.astype(jnp.int32), jnp.where(tick < LAG, jnp.minimum((tick + 1) * early, M), 0))
    lax.fori_loop(pos_from, pos_to, position, 0)

    def forward():
        base = pl.multiple_of(f_chunk * R, 16)
        cloud0 = f_chunk * C
        here = pl.ds(base, R)

        @pl.when(role == 0)
        def _():
            X[...] = jnp.zeros(X.shape, F32)
            memb = r["memb"][...].astype(F32)
            for c in range(C):
                hit = masked_rows(r["mask_idx"], cloud0 + c, PR)[:rows_in]
                tok = r["tokens"][cloud0 + c].astype(F32)
                X[pl.ds(c * PR, rows_in), :] = jnp.where(hit, memb, tok)

        @pl.when(role != 0)
        def _():
            X[...] = r["recv"][...].astype(F32)

        h = X[...] + dot(r["pc"][here, :], r["pw2"][...]) + r["pb2"][...]
        H[...] = h
        vh1, rs1 = norm_stats(h)
        r["rs1"][here, :] = rs1
        r["vh1"][here, :] = vh1.astype(BF16)
        n1 = (vh1 * r["gain"][0:1] + r["bias"][0:1]).astype(BF16)
        r["n1"][here, :] = n1
        for col in col_chunks(3 * D, QKV_COLS):
            qkv = dot(n1, r["qkv_w"][:, col]).astype(BF16)
            r["qkv"][here, col] = qkv
            Q[:, col] = qkv.astype(F32)
        for c in range(C):
            at = pl.ds(c * PR, PR)
            for j in range(pairs):
                q = Q[at, pl.ds(j * LANES, LANES)] * scale
                k = Q[at, pl.ds(D + j * LANES, LANES)].astype(BF16)
                S[pl.ds((c * pairs + j) * 2 * PR, 2 * PR), :] = dot_t(stack_heads(q, low).astype(BF16), k)
        key_ok = lax.broadcasted_iota(jnp.int32, (2 * PR, PR), 1) < rows_in
        for i in range(C * pairs):
            s = jnp.where(key_ok, S[pl.ds(i * 2 * PR, 2 * PR), :], -1e30)
            e = jnp.exp(s - jnp.max(s, axis=1, keepdims=True))
            p = e * pl.reciprocal(jnp.sum(e, axis=1, keepdims=True))
            r["p"][pl.ds(pl.multiple_of((cloud0 * pairs + i) * 2 * PR, 16), 2 * PR), :] = p.astype(BF16)
        for c in range(C):
            at = pl.ds(c * PR, PR)
            for j in range(pairs):
                i = cloud0 * pairs + c * pairs + j
                v = Q[at, pl.ds(2 * D + j * LANES, LANES)].astype(BF16)
                p = r["p"][pl.ds(pl.multiple_of(i * 2 * PR, 16), 2 * PR), :]
                O[at, pl.ds(j * LANES, LANES)] = merge_heads(dot(p, v), low)
        o = O[...].astype(BF16)
        r["o"][here, :] = o
        res = H[...] + dot(o, r["proj_w"][...]) + r["ob"][0:1]
        vh2, rs2 = norm_stats(res)
        r["rs2"][here, :] = rs2
        r["vh2"][here, :] = vh2.astype(BF16)
        n2 = (vh2 * r["gain"][1:2] + r["bias"][1:2]).astype(BF16)
        r["n2"][here, :] = n2
        H[...] = res + r["ob"][1:2]
        for col in col_chunks(FF, F_COLS):
            u, gu = gelu_pair(dot(n2, r["fc1_w"][:, col]) + r["fc1_b"][:, col])
            u = u.astype(BF16)
            r["u"][here, col] = u
            r["gu"][here, col] = gu.astype(BF16)
            H[...] += dot(u, r["fc2_w"][col, :])
        y = H[...].astype(BF16)
        r["yb"][here, :] = y

        @pl.when(role == 0)
        def _():
            r["send"][...] = y

    def backward():
        base = pl.multiple_of(g_chunk * R, 16)
        cloud0 = g_chunk * C
        here = pl.ds(base, R)
        small = r["small"]

        @pl.when(role != 0)
        def _():
            X[...] = jnp.zeros(X.shape, F32)
            for c in range(C):
                X[pl.ds(c * PR, rows_in), :] = r["cot"][cloud0 + c].astype(F32)

        @pl.when(role == 0)
        def _():
            X[...] = r["recv"][...].astype(F32)

        dy = X[...]
        dyb = dy.astype(BF16)
        r["dyb"][here, :] = dyb
        small[2:3, pl.ds(D, D)] += colsum(dy)
        for j, col in enumerate(col_chunks(FF, G_COLS)):
            df = dot_t(dyb, r["fc2_w"][col, :]) * r["gu"][here, col].astype(F32)
            small[0:1, col] += colsum(df)
            dfb = df.astype(BF16)
            r["gu"][here, col] = dfb
            part = dot_t(dfb, r["fc1_w"][:, col])
            if j == 0:
                H[...] = part
            else:
                H[...] += part
        dn2 = H[...]
        vh2 = r["vh2"][here, :].astype(F32)
        small[1:2, pl.ds(D, D)] += colsum(dn2 * vh2)
        small[1:2, pl.ds(3 * D, D)] += colsum(dn2)
        dr = X[...] + norm_back(dn2, r["gain"][1:2], vh2, r["rs2"][here, :])
        X[...] = dr
        small[2:3, pl.ds(0, D)] += colsum(dr)
        drb = dr.astype(BF16)
        r["vh2"][here, :] = drb
        G[...] = dot_t(drb, r["proj_w"][...]).astype(BF16).astype(F32)
        Q[...] = r["qkv"][here, :].astype(F32)

        units = [(c, j) for c in range(C) for j in range(pairs)]

        def p_of(c, j):
            i = (cloud0 + c) * pairs + j
            return r["p"][pl.ds(pl.multiple_of(i * 2 * PR, 16), 2 * PR), :]

        def do_of(c, j):
            return stack_heads(G[pl.ds(c * PR, PR), pl.ds(j * LANES, LANES)], low).astype(BF16)

        for i, (c, j) in enumerate(units):
            v = Q[pl.ds(c * PR, PR), pl.ds(2 * D + j * LANES, LANES)].astype(BF16)
            S[pl.ds(i * 2 * PR, 2 * PR), :] = dot_t(do_of(c, j), v)
        for i, (c, j) in enumerate(units):
            p = p_of(c, j).astype(F32)
            dp = S[pl.ds(i * 2 * PR, 2 * PR), :]
            ds = p * (dp - jnp.sum(dp * p, axis=1, keepdims=True))
            S[pl.ds(i * 2 * PR, 2 * PR), :] = ds * scale
        for i, (c, j) in enumerate(units):
            at = pl.ds(c * PR, PR)
            q_at, k_at, v_at = (pl.ds(n * D + j * LANES, LANES) for n in range(3))
            q = stack_heads(Q[at, q_at], low).astype(BF16)
            k = Q[at, k_at].astype(BF16)
            dsb = S[pl.ds(i * 2 * PR, 2 * PR), :].astype(BF16)
            dq = merge_heads(dot(dsb, k), low)
            dk = dot_c(dsb, q)
            Q[at, v_at] = dot_c(p_of(c, j), do_of(c, j))
            Q[at, q_at] = dq
            Q[at, k_at] = dk
        for j, col in enumerate(col_chunks(3 * D, QKV_COLS)):
            dq = Q[:, col].astype(BF16)
            r["qkv"][here, col] = dq
            part = dot_t(dq, r["qkv_w"][:, col])
            if j == 0:
                H[...] = part
            else:
                H[...] += part
        dn1 = H[...]
        vh1 = r["vh1"][here, :].astype(F32)
        small[1:2, pl.ds(0, D)] += colsum(dn1 * vh1)
        small[1:2, pl.ds(2 * D, D)] += colsum(dn1)
        dh = X[...] + norm_back(dn1, r["gain"][0:1], vh1, r["rs1"][here, :])
        X[...] = dh
        small[2:3, pl.ds(2 * D, D)] += colsum(dh)
        dhb = dh.astype(BF16)
        r["vh1"][here, :] = dhb
        O[:, :LANES] = dot_t(dhb, r["pw2"][...]) * r["gz"][here, :].astype(F32)
        for c in range(C):
            cen = centre_rows(r["centers"], cloud0 + c)
            dz = O[pl.ds(c * PR, PR), :LANES]
            dz = jnp.concatenate([dz, jnp.zeros((LANES - PR, LANES), F32)], axis=0)
            dw = dot_f32(cen, dz)
            for i in range(4):
                small[3:4, pl.ds(i * LANES, LANES)] += dw[i : i + 1]

        @pl.when(role != 0)
        def _():
            r["dx"][here, :] = X[...]
            r["send"][...] = dhb

        @pl.when(role == 0)
        def _():
            for c in range(C):
                hit = masked_rows(r["mask_idx"], cloud0 + c, PR)
                at = pl.ds(c * PR, PR)
                dx = X[at, :]
                r["dx"][pl.ds(pl.multiple_of(base + c * PR, 8), PR), :] = jnp.where(hit, 0.0, dx)
                small[2:3, pl.ds(3 * D, D)] += colsum(jnp.where(hit, dx, 0.0))

    pl.when(f_on)(forward)
    pl.when(g_on)(backward)


def vmem(x):
    return pltpu.with_memory_space_constraint(x, pltpu.VMEM)


def blocked_product(left_ref, right_ref, out_ref, at):
    height = left_ref.shape[1]
    step = min(height, 384)
    for i in range(0, height, step):
        block = dot_c(left_ref[:, pl.ds(i, step)], right_ref[...]).astype(BF16)
        for j in range(right_ref.shape[1] // LANES):
            out_ref[pl.ds(at + j * height + i, step), :] = block[:, j * LANES : (j + 1) * LANES]
    return at + height * right_ref.shape[1] // LANES


def wgrad_kernel(left_ref, right_ref, out_ref):
    blocked_product(left_ref, right_ref, out_ref, 0)


def rest_kernel(position, o, drb, pc, dhb, small, small_got, out_ref):
    at = blocked_product(o, drb, out_ref, 0)
    at = blocked_product(pc, dhb, out_ref, at)
    width = small.shape[1]
    mask_at = 3 * width // 4
    rows = []
    for i in range(4):
        for j in range(0, width, LANES):
            row = small[i : i + 1, j : j + LANES]
            if i == 2 and j >= mask_at:
                row = jnp.where(position[0] == 0, row, small_got[i : i + 1, j : j + LANES])
            rows.append(row)
    out_ref[pl.ds(at, len(rows)), :] = jnp.concatenate(rows, axis=0).astype(BF16)
    at += len(rows)
    if at < out_ref.shape[0]:
        out_ref[pl.ds(at, out_ref.shape[0] - at), :] = jnp.zeros((out_ref.shape[0] - at, LANES), BF16)


def weight_grad(left, right, name):
    k, m = left.shape
    n = right.shape[1]
    whole = pl.BlockSpec(memory_space=pltpu.VMEM)
    return pl.pallas_call(
        wgrad_kernel,
        out_shape=jax.ShapeDtypeStruct((m * n // LANES, LANES), BF16),
        in_specs=[whole] * 2,
        out_specs=whole,
        compiler_params=pltpu.CompilerParams(vmem_limit_bytes=VMEM_LIMIT),
        cost_estimate=pl.CostEstimate(flops=2 * k * m * n, bytes_accessed=2 * (k * m + k * n), transcendentals=0),
        name=name,
    )(vmem(left), vmem(right))


def reduce_steps(n):
    steps = [(1 << b, 1 << b) for b in range(n.bit_length() - 1)]
    if len(steps) >= 3:
        steps[1], steps[2] = (2, 4), (4, 2)
    return steps


def swap(x, masks, n):
    return lax.ppermute(x, "dp", [(i, i ^ masks[i & 1]) for i in range(n)])


def upper(me, masks):
    mask = jnp.where(me & 1, masks[1], masks[0])
    return ((me & mask) != 0).astype(jnp.int32)


def halve(buf, masks, me, n):
    half = buf.shape[0] // 2
    bit = upper(me, masks)
    send = lax.dynamic_slice_in_dim(buf, (1 - bit) * half, half, 0)
    keep = lax.dynamic_slice_in_dim(buf, bit * half, half, 0)
    got = swap(send, masks, n)
    return (keep.astype(F32) + got.astype(F32)).astype(BF16)


def double(buf, masks, me, n):
    bit = upper(me, masks)
    got = swap(buf, masks, n)
    return jnp.concatenate([jnp.where(bit == 0, buf, got), jnp.where(bit == 0, got, buf)], axis=0)


def sum_over_dp(bufs, me):
    n = lax.axis_size("dp")
    if n & (n - 1):
        return [lax.psum(b, "dp") for b in bufs]
    steps = reduce_steps(n)
    bufs = list(bufs)
    total = 2 * len(steps)
    for t in range(total + len(bufs) - 1):
        for g in range(len(bufs)):
            s = t - g
            if 0 <= s < len(steps):
                bufs[g] = halve(bufs[g], steps[s], me, n)
            elif len(steps) <= s < total:
                bufs[g] = double(bufs[g], steps[total - 1 - s], me, n)
    return bufs


def unblock(buf, rows):
    blocks = buf.shape[0] // rows
    return jnp.concatenate([buf[j * rows : (j + 1) * rows] for j in range(blocks)], axis=1).astype(F32)


def shards(
    tokens,
    mask_emb,
    mask_idx,
    centers,
    cotangent,
    ln_gain,
    ln_bias,
    qkv_w,
    proj_w,
    out_bias,
    fc1_w,
    fc1_b,
    fc2_w,
    pos_w1,
    pos_b1,
    pos_w2,
    pos_b2,
):
    M, C, rows_in, D = tokens.shape
    FF = fc1_w.shape[2]
    PR = -(-rows_in // 8) * 8
    R = C * PR
    total = M * R
    role = lax.axis_index("section")
    clouds = M * C
    base_args = [
        tokens.reshape(clouds, rows_in, D),
        mask_emb.reshape(1, D),
        mask_idx.reshape(clouds, -1),
        centers.reshape(3, clouds, -1),
        cotangent.reshape(clouds, rows_in, D),
        ln_gain[0],
        ln_bias[0],
        qkv_w[0],
        proj_w[0],
        out_bias[0],
        fc1_w[0],
        fc1_b.reshape(1, FF),
        fc2_w[0],
        pos_w1[0],
        pos_b1.reshape(1, -1),
        pos_w2[0],
        pos_b2.reshape(1, D),
    ]
    base_args = [vmem(a) for a in base_args]
    buf_shapes = [((total, w * LANES), dt) for _, w, dt in SAVES]
    buf_shapes += [
        ((clouds * HEADS * PR, PR), BF16),
        ((total, 1), F32),
        ((total, 1), F32),
        ((total, D), F32),
        ((8, FF), F32),
    ]
    send_shape = ((R, D), BF16)
    cfg = (M, C, rows_in, PR, D, FF)
    whole = pl.BlockSpec(memory_space=pltpu.VMEM)
    position = jnp.stack([role, lax.axis_index("dp")]).astype(jnp.int32)
    *bufs, blank = pl.pallas_call(
        alloc_kernel,
        out_shape=[pltpu.VMEM(s, d) for s, d in buf_shapes + [send_shape]],
        in_specs=[pl.BlockSpec(memory_space=pltpu.SMEM)] + [whole] * len(base_args),
        out_specs=[whole] * (len(buf_shapes) + 1),
        compiler_params=pltpu.CompilerParams(vmem_limit_bytes=VMEM_LIMIT),
        name="alloc",
    )(position, *base_args)

    def tick(t, bufs, recv):
        args = [jnp.array([t], jnp.int32), position] + base_args + [vmem(recv)] + [vmem(b) for b in bufs]
        n_in = len(args)
        outs = pl.pallas_call(
            functools.partial(tick_kernel, cfg),
            out_shape=[pltpu.VMEM(s, d) for s, d in buf_shapes + [send_shape]],
            in_specs=[pl.BlockSpec(memory_space=pltpu.SMEM)] * 2 + [whole] * (n_in - 2),
            out_specs=[whole] * (len(buf_shapes) + 1),
            scratch_shapes=[
                pltpu.VMEM((R, D), F32),
                pltpu.VMEM((R, D), F32),
                pltpu.VMEM((R, 3 * D), F32),
                pltpu.VMEM((R, D), F32),
                pltpu.VMEM((R, D), F32),
                pltpu.VMEM((C * HEADS * PR, PR), F32),
            ],
            input_output_aliases={n_in - len(bufs) + i: i for i in range(len(bufs))},
            compiler_params=pltpu.CompilerParams(vmem_limit_bytes=VMEM_LIMIT),
            cost_estimate=pl.CostEstimate(flops=4 * 10**9, bytes_accessed=10**6, transcendentals=0),
            name="tick",
        )(*args)
        return list(outs[:-1]), outs[-1]

    sections = lax.axis_size("section")
    swap_sections = [(i, sections - 1 - i) for i in range(sections)]
    sent = []
    for t in range(M + 2 * LAG):
        recv = lax.ppermute(sent[t - LAG], "section", swap_sections) if t >= LAG else blank
        bufs, send = tick(t, bufs, recv)
        sent.append(send)
    b = dict(zip([s[0] for s in SAVES] + ["p", "rs1", "rs2", "dx", "small"], bufs, strict=True))

    small_got = lax.ppermute(b["small"], "section", swap_sections)
    fc2_part = weight_grad(b["u"], b["dyb"], "wgrad_fc2")
    fc1_part = weight_grad(b["n2"], b["gu"], "wgrad_fc1")
    qkv_part = weight_grad(b["n1"], b["qkv"], "wgrad_qkv")
    n_proj, n_pos, n_small = D * D // LANES, D, 4 * FF // LANES
    height = -(-(n_proj + n_pos + n_small) // 256) * 256
    rest = pl.pallas_call(
        rest_kernel,
        out_shape=jax.ShapeDtypeStruct((height, LANES), BF16),
        in_specs=[pl.BlockSpec(memory_space=pltpu.SMEM)] + [whole] * 6,
        out_specs=whole,
        compiler_params=pltpu.CompilerParams(vmem_limit_bytes=VMEM_LIMIT),
        name="wgrad_rest",
    )(position, *[vmem(x) for x in (b["o"], b["vh2"], b["pc"], b["vh1"], b["small"], small_got)])
    fc2_part, fc1_part, qkv_part, rest, yb, dx, position = lax.optimization_barrier(
        (fc2_part, fc1_part, qkv_part, rest, b["yb"], b["dx"], position)
    )
    me = position[1]
    fc2_sum, fc1_sum, qkv_sum, rest_sum = sum_over_dp([fc2_part, fc1_part, qkv_part, rest], me)

    fc2_g = unblock(fc2_sum, FF)
    fc1_g = unblock(fc1_sum, D)
    qkv_g = unblock(qkv_sum, D)
    proj_g = unblock(rest_sum[:n_proj], D)
    pos_g = unblock(rest_sum[n_proj : n_proj + n_pos], LANES)
    sm = rest_sum[n_proj + n_pos : n_proj + n_pos + n_small].astype(F32).reshape(-1)
    cuts = [FF, 2 * D, 2 * D, 2 * D, D, D, 3 * LANES, LANES, FF - 4 * LANES]
    at = 0
    got = []
    for c in cuts:
        got.append(sm[at : at + c])
        at += c
    fc1_b_g, gain_g, bias_g, ob_g, pb2_g, mask_g, pw1_g, pb1_g = got[:-1]
    section_out = yb.reshape(M, C, PR, D)[:, :, :rows_in]
    section_grad = dx.reshape(M, C, PR, D)[:, :, :rows_in]
    return (
        section_out[None],
        section_grad[None],
        mask_g,
        gain_g.reshape(1, 2, D),
        bias_g.reshape(1, 2, D),
        qkv_g[None],
        proj_g[None],
        ob_g.reshape(1, 2, D),
        fc1_g[None],
        fc1_b_g[None],
        fc2_g[None],
        pw1_g.reshape(1, 3, LANES),
        pb1_g[None],
        pos_g[None],
        pb2_g[None],
    )


def solution(mesh):
    return jax.shard_map(
        shards,
        mesh=mesh,
        in_specs=(
            P(None, "dp", None, None),
            P(),
            P(None, "dp", None),
            P(None, None, "dp", None),
            P(None, "dp", None, None),
            P("section", None, None),
            P("section", None, None),
            P("section", None, None),
            P("section", None, None),
            P("section", None, None),
            P("section", None, None),
            P("section", None),
            P("section", None, None),
            P("section", None, None),
            P("section", None),
            P("section", None, None),
            P("section", None),
        ),
        out_specs=(
            P("section", None, "dp", None, None),
            P("section", None, "dp", None, None),
            P(),
            P("section", None, None),
            P("section", None, None),
            P("section", None, None),
            P("section", None, None),
            P("section", None, None),
            P("section", None, None),
            P("section", None),
            P("section", None, None),
            P("section", None, None),
            P("section", None),
            P("section", None, None),
            P("section", None),
        ),
        check_vma=False,
    )
```

```python
import functools
import math

import jax
import jax.numpy as jnp
from jax import lax
from jax.experimental import pallas as pl
from jax.experimental.pallas import tpu as pltpu
from jax.sharding import PartitionSpec as P

HEADS = 6
HD = 64
EPS = 1e-05
LANES = 128
MIB = 1 << 20
TICK_UNITS = (1, 1, 1, 1, 1, 1)
LAG = 2
QKV_COLS = 768
HID = 256
SUB = 288
HALF = 288
GW = 1536
GQ = 768
PHASES = True
VMEM_LIMIT = 12 * MIB

F32 = jnp.float32
BF16 = jnp.bfloat16

ERF_P = 0.375
ERF_C = (
    0.21137403,
    0.21522517,
    0.16911028,
    0.27655959,
    -0.12036233,
    0.3812622,
    -0.1331683,
)
ROOT_HALF = 0.7071067811865476
HALF_LOG2_E = -0.7213475204444817
INV_ROOT_TWO_PI = 0.3989422804014327


def gelu_pair(f):
    den = 1.0 + (ERF_P * ROOT_HALF) * jnp.abs(f)
    t = pl.reciprocal(den, approx=True)
    e = jnp.exp2((f * f) * HALF_LOG2_E)
    poly = 0.5 * ERF_C[-1]
    for c in ERF_C[-2::-1]:
        poly = poly * t + 0.5 * c
    q = e * (t * poly)
    cdf = jnp.where(f >= 0, 1.0 - q, q)
    return f * cdf, cdf + f * (INV_ROOT_TWO_PI * e)


def dot(a, b):
    return jnp.dot(a, b, preferred_element_type=F32)


def dot_t(a, b):
    return lax.dot_general(a, b, (((1,), (1,)), ((), ())), preferred_element_type=F32)


def dot_c(a, b):
    return lax.dot_general(a, b, (((0,), (0,)), ((), ())), preferred_element_type=F32)


def dot_c_f32(a, b):
    return lax.dot_general(
        a, b, (((0,), (0,)), ((), ())), preferred_element_type=F32, precision=lax.Precision.HIGHEST
    )


def dot_f32(a, b):
    return jnp.dot(a, b, preferred_element_type=F32, precision=lax.Precision.HIGHEST)


def centre_rows(centers_ref, cloud):
    patch_count = centers_ref.shape[2]
    rows = [centers_ref[i, pl.ds(cloud, 1), :] for i in range(3)]
    body = jnp.concatenate(rows, axis=0)
    body = jnp.concatenate([jnp.zeros((3, 1), F32), body], axis=1)
    body = jnp.concatenate([body, jnp.zeros((3, LANES - 1 - patch_count), F32)], axis=1)
    return jnp.concatenate([body, jnp.ones((1, LANES), F32), jnp.zeros((4, LANES), F32)], axis=0)


def masked_rows(mask_idx_ref, cloud, padded):
    ids = mask_idx_ref[pl.ds(cloud, 1), :]
    rows = lax.broadcasted_iota(jnp.int32, (padded, ids.shape[1]), 0) - 1
    return jnp.max((rows == ids).astype(F32), axis=1, keepdims=True) > 0.0


def norm_stats(v):
    width = v.shape[1]
    mean = jnp.sum(v, axis=1, keepdims=True) * (1.0 / width)
    cen = v - mean
    var = jnp.sum(cen * cen, axis=1, keepdims=True) * (1.0 / width)
    rs = lax.rsqrt(var + EPS)
    return cen * rs, rs


def norm_back(dn, gain, vhat, rs):
    width = dn.shape[1]
    dg = dn * gain
    m1 = jnp.sum(dg, axis=1, keepdims=True) * (1.0 / width)
    m2 = jnp.sum(dg * vhat, axis=1, keepdims=True) * (1.0 / width)
    return rs * (dg - m1 - vhat * m2)


def colsum(v):
    return jnp.sum(v, axis=0, keepdims=True)


def stack_heads(pair, low):
    zero = jnp.zeros_like(pair)
    return jnp.concatenate([jnp.where(low, pair, zero), jnp.where(low, zero, pair)], axis=0)


def merge_heads(stacked, low):
    n = stacked.shape[0] // 2
    return jnp.where(low, stacked[:n], stacked[n:])


SAVES = (
    ("pc", 1, BF16),
    ("gz", 1, BF16),
    ("vh1", 3, BF16),
    ("n1", 3, BF16),
    ("qkv", 9, BF16),
    ("o", 3, BF16),
    ("vh2", 3, BF16),
    ("n2", 3, BF16),
    ("u", 12, BF16),
    ("gu", 12, BF16),
    ("dyb", 3, BF16),
    ("yb", 3, BF16),
)


def alloc_kernel(*refs):
    for ref in refs[-2:]:
        ref[...] = jnp.zeros(ref.shape, ref.dtype)


def tick_kernel(cfg, plan, *refs):
    (C, rows_in, PR, D, FF) = cfg
    R = C * PR
    names = ["position", "tokens", "memb", "mask_idx", "centers", "cot"]
    names += ["gain", "bias", "qkv_w", "proj_w", "ob", "fc1_w", "fc1_b", "fc2_w", "pw1", "pb1", "pw2", "pb2"]
    names += ["recv"]
    buf_names = [s[0] for s in SAVES] + ["p", "rs1", "rs2", "dx", "small"]
    names += ["old_" + b for b in buf_names]
    names += buf_names + ["send"]
    scratch_names = ["X", "H", "Q", "O", "G", "S", "FA", "FB"]
    names += scratch_names
    r = dict(zip(names, refs, strict=True))
    role = r["position"][0]
    first = role == 0
    pairs = HEADS // 2
    low = lax.broadcasted_iota(jnp.int32, (PR, LANES), 1) < HD
    scale = HD**-0.5
    X, H, Q, O, G, S, FA, FB = (r[s] for s in scratch_names)
    small = r["small"]
    units = [(c, j) for c in range(C) for j in range(pairs)]
    chunks = FF // HID

    def run(which, body):
        (from0, count0), (from1, count1) = plan[0][which], plan[1][which]
        if count0 == count1 == 0:
            return
        start = jnp.where(first, from0, from1)
        count = jnp.where(first, count0, count1)

        def step(k, carry):
            body(start + k, k)
            return carry

        lax.fori_loop(0, count, step, 0)

    def rows_of(c):
        return pl.ds(c * PR, PR)

    def unit_rows(unit, i):
        return pl.ds(pl.multiple_of((unit * C * pairs + i) * 2 * PR, 16), 2 * PR)

    def scores(i):
        return pl.ds(i * 2 * PR, 2 * PR)

    def cols(j):
        return pl.ds(j * HID, HID)

    def staged(stages, count):
        for i in range(count + len(stages) - 1):
            for lag, stage in enumerate(stages):
                if 0 <= i - lag < count:
                    stage(i - lag)

    def position(unit, k):
        here = pl.ds(pl.multiple_of(unit * R, 16), R)
        w1 = jnp.concatenate([r["pw1"][...], r["pb1"][...], jnp.zeros((4, LANES), F32)], axis=0)
        for c in range(C):
            O[rows_of(c), :LANES] = dot_c_f32(centre_rows(r["centers"], unit * C + c), w1)[:PR]
        pc, gz = gelu_pair(O[:, :LANES])
        r["pc"][here, :] = pc.astype(BF16)
        r["gz"][here, :] = gz.astype(BF16)

    def forward(unit, k):
        base = pl.multiple_of(unit * R, 16)
        cloud0 = unit * C
        here = pl.ds(base, R)
        mail = pl.ds(pl.multiple_of(k * R, 16), R)

        def saved(at, count):
            return pl.ds(pl.multiple_of(base + at, 16), count)

        @pl.when(first)
        def _():
            X[...] = jnp.zeros(X.shape, F32)
            memb = r["memb"][...].astype(F32)
            for c in range(C):
                hit = masked_rows(r["mask_idx"], cloud0 + c, PR)[:rows_in]
                tok = r["tokens"][cloud0 + c].astype(F32)
                X[pl.ds(c * PR, rows_in), :] = jnp.where(hit, memb, tok)

        @pl.when(role != 0)
        def _():
            X[...] = r["recv"][mail, :].astype(F32)

        H[...] = X[...] + dot(r["pc"][here, :], r["pw2"][...]) + r["pb2"][...]
        for at in range(0, R, SUB):
            vh1, rs1 = norm_stats(H[pl.ds(at, SUB), :])
            r["rs1"][saved(at, SUB), :] = rs1
            r["vh1"][saved(at, SUB), :] = vh1.astype(BF16)
            r["n1"][saved(at, SUB), :] = (vh1 * r["gain"][0:1] + r["bias"][0:1]).astype(BF16)
        for at in range(0, 3 * D, QKV_COLS):
            col = pl.ds(at, min(QKV_COLS, 3 * D - at))
            qkv = dot(r["n1"][here, :], r["qkv_w"][:, col]).astype(BF16)
            r["qkv"][here, col] = qkv
            Q[:, col] = qkv.astype(F32)
        key_ok = lax.broadcasted_iota(jnp.int32, (2 * PR, PR), 1) < rows_in

        def score(i):
            c, j = units[i]
            q = Q[rows_of(c), pl.ds(j * LANES, LANES)] * scale
            k = Q[rows_of(c), pl.ds(D + j * LANES, LANES)].astype(BF16)
            S[scores(i), :] = dot_t(stack_heads(q, low).astype(BF16), k)

        def soften(i):
            s = jnp.where(key_ok, S[scores(i), :], -1e30)
            e = jnp.exp(s - jnp.max(s, axis=1, keepdims=True))
            p = (e * pl.reciprocal(jnp.sum(e, axis=1, keepdims=True))).astype(BF16)
            r["p"][unit_rows(unit, i), :] = p

        def weigh(i):
            c, j = units[i]
            v = Q[rows_of(c), pl.ds(2 * D + j * LANES, LANES)].astype(BF16)
            o = merge_heads(dot(r["p"][unit_rows(unit, i), :], v), low)
            O[rows_of(c), pl.ds(j * LANES, LANES)] = o

        if PHASES:
            for stage in (score, soften, weigh):
                staged([stage], len(units))
        else:
            staged([score, soften, weigh], len(units))
        o = O[...].astype(BF16)
        r["o"][here, :] = o
        H[...] += dot(o, r["proj_w"][...]) + r["ob"][0:1]
        for at in range(0, R, SUB):
            res = H[pl.ds(at, SUB), :]
            vh2, rs2 = norm_stats(res)
            r["rs2"][saved(at, SUB), :] = rs2
            r["vh2"][saved(at, SUB), :] = vh2.astype(BF16)
            r["n2"][saved(at, SUB), :] = (vh2 * r["gain"][1:2] + r["bias"][1:2]).astype(BF16)
            H[pl.ds(at, SUB), :] = res + r["ob"][1:2]

        def enter(i):
            j, part = divmod(i, R // HALF)
            buf = (FA, FB)[j % 2]
            n2 = r["n2"][saved(part * HALF, HALF), :]
            buf[pl.ds(part * HALF, HALF), :] = dot(n2, r["fc1_w"][:, cols(j)]) + r["fc1_b"][:, cols(j)]

        def leave(i):
            j, part = divmod(i, R // HALF)
            buf = (FA, FB)[j % 2]
            for at in range(part * HALF, (part + 1) * HALF, SUB):
                u, gu = gelu_pair(buf[pl.ds(at, SUB), :])
                r["u"][saved(at, SUB), cols(j)] = u.astype(BF16)
                r["gu"][saved(at, SUB), cols(j)] = gu.astype(BF16)

        def close(i):
            j, part = divmod(i, R // HALF)
            H[pl.ds(part * HALF, HALF), :] += dot(r["u"][saved(part * HALF, HALF), cols(j)], r["fc2_w"][cols(j), :])

        staged([enter, leave, close], chunks * R // HALF)
        y = H[...].astype(BF16)
        r["yb"][here, :] = y

        @pl.when(first)
        def _():
            r["send"][mail, :] = y

    def backward(unit, k):
        base = pl.multiple_of(unit * R, 16)
        cloud0 = unit * C
        here = pl.ds(base, R)
        mail = pl.ds(pl.multiple_of(k * R, 16), R)

        def saved(at, count):
            return pl.ds(pl.multiple_of(base + at, 16), count)

        @pl.when(role != 0)
        def _():
            X[...] = jnp.zeros(X.shape, F32)
            for c in range(C):
                X[pl.ds(c * PR, rows_in), :] = r["cot"][cloud0 + c].astype(F32)

        @pl.when(first)
        def _():
            X[...] = r["recv"][mail, :].astype(F32)

        r["dyb"][here, :] = X[...].astype(BF16)
        small[2:3, pl.ds(D, D)] += colsum(X[...])

        for at in range(0, FF, GW):
            col = pl.ds(at, GW)
            df = dot_t(r["dyb"][here, :], r["fc2_w"][col, :]) * r["gu"][here, col].astype(F32)
            small[0:1, col] += colsum(df)
            dfb = df.astype(BF16)
            r["gu"][here, col] = dfb
            part = dot_t(dfb, r["fc1_w"][:, col])
            H[...] = part if at == 0 else H[...] + part
        sums = [0.0] * 3
        for at in range(0, R, SUB):
            rows = pl.ds(at, SUB)
            dn2 = H[rows, :]
            vh2 = r["vh2"][saved(at, SUB), :].astype(F32)
            dr = X[rows, :] + norm_back(dn2, r["gain"][1:2], vh2, r["rs2"][saved(at, SUB), :])
            X[rows, :] = dr
            r["vh2"][saved(at, SUB), :] = dr.astype(BF16)
            sums = [s + colsum(v) for s, v in zip(sums, (dn2 * vh2, dn2, dr))]
        for row, at, s in zip((1, 1, 2), (D, 3 * D, 0), sums):
            small[row : row + 1, pl.ds(at, D)] += s
        G[...] = dot_t(r["vh2"][here, :], r["proj_w"][...]).astype(BF16).astype(F32)
        Q[...] = r["qkv"][here, :].astype(F32)

        def do_of(i):
            c, j = units[i]
            return stack_heads(G[rows_of(c), pl.ds(j * LANES, LANES)], low).astype(BF16)

        def score(i):
            c, j = units[i]
            v = Q[rows_of(c), pl.ds(2 * D + j * LANES, LANES)].astype(BF16)
            S[scores(i), :] = dot_t(do_of(i), v)

        def soften(i):
            p = r["p"][unit_rows(unit, i), :].astype(F32)
            dp = S[scores(i), :]
            ds = p * (dp - jnp.sum(dp * p, axis=1, keepdims=True))
            S[scores(i), :] = ds * scale

        def weigh(i):
            c, j = units[i]
            at = rows_of(c)
            q_at, k_at, v_at = (pl.ds(m * D + j * LANES, LANES) for m in range(3))
            q = stack_heads(Q[at, q_at], low).astype(BF16)
            k = Q[at, k_at].astype(BF16)
            dsb = S[scores(i), :].astype(BF16)
            dq = merge_heads(dot(dsb, k), low)
            dk = dot_c(dsb, q)
            Q[at, v_at] = dot_c(r["p"][unit_rows(unit, i), :], do_of(i))
            Q[at, q_at] = dq
            Q[at, k_at] = dk

        if PHASES:
            for stage in (score, soften, weigh):
                staged([stage], len(units))
        else:
            staged([score, soften, weigh], len(units))
        for at in range(0, 3 * D, GQ):
            col = pl.ds(at, min(GQ, 3 * D - at))
            dqkv = Q[:, col].astype(BF16)
            r["qkv"][here, col] = dqkv
            part = dot_t(dqkv, r["qkv_w"][:, col])
            H[...] = part if at == 0 else H[...] + part
        sums = [0.0] * 3
        for at in range(0, R, SUB):
            rows = pl.ds(at, SUB)
            dn1 = H[rows, :]
            vh1 = r["vh1"][saved(at, SUB), :].astype(F32)
            dh = X[rows, :] + norm_back(dn1, r["gain"][0:1], vh1, r["rs1"][saved(at, SUB), :])
            X[rows, :] = dh
            r["vh1"][saved(at, SUB), :] = dh.astype(BF16)
            sums = [s + colsum(v) for s, v in zip(sums, (dn1 * vh1, dn1, dh))]
        for row, at, s in zip((1, 1, 2), (0, 2 * D, 2 * D), sums):
            small[row : row + 1, pl.ds(at, D)] += s
        dhb = r["vh1"][here, :]

        @pl.when(role != 0)
        def _():
            r["send"][mail, :] = dhb

        O[:, :LANES] = dot_t(dhb, r["pw2"][...]) * r["gz"][here, :].astype(F32)
        for c in range(C):
            cen = centre_rows(r["centers"], cloud0 + c)
            dz = jnp.concatenate([O[rows_of(c), :LANES], jnp.zeros((LANES - PR, LANES), F32)], axis=0)
            dw = dot_f32(cen, dz)
            for i in range(4):
                small[3:4, pl.ds(i * LANES, LANES)] += dw[i : i + 1]
            dx_at = pl.ds(pl.multiple_of(base + c * PR, 8), PR)

            @pl.when(first)
            def _():
                hit = masked_rows(r["mask_idx"], cloud0 + c, PR)
                dx = X[rows_of(c), :]
                r["dx"][dx_at, :] = jnp.where(hit, 0.0, dx)
                small[2:3, pl.ds(3 * D, D)] += colsum(jnp.where(hit, dx, 0.0))

            @pl.when(role != 0)
            def _():
                r["dx"][dx_at, :] = X[rows_of(c), :]

    run(0, position)
    run(1, forward)
    run(2, backward)


def tick_units(units):
    if sum(TICK_UNITS) == units:
        return TICK_UNITS
    return (1,) * units


def tick_plan(chunks, t, units):
    none = (0, 0)

    def chunk(i):
        return chunks[i] if 0 <= i < len(chunks) else none

    half = -(-units // LAG)
    early = (t * half, min(half, units - t * half)) if t < LAG else none
    return (chunk(t), chunk(t), chunk(t - 2 * LAG)), (early, chunk(t - LAG), chunk(t - LAG))


def tick_scratch(cfg):
    (C, _, PR, D, _) = cfg
    R = C * PR
    wide = [(R, D), (R, D), (R, 3 * D), (R, D), (R, D), (C * HEADS * PR, PR), (R, HID), (R, HID)]
    return [pltpu.VMEM(shape, F32) for shape in wide]


def vmem(x):
    return pltpu.with_memory_space_constraint(x, pltpu.VMEM)


def blocked_product(left_ref, right_ref, out_ref, at):
    height = left_ref.shape[1]
    step = min(height, 384)
    for i in range(0, height, step):
        block = dot_c(left_ref[:, pl.ds(i, step)], right_ref[...]).astype(BF16)
        for j in range(right_ref.shape[1] // LANES):
            out_ref[pl.ds(at + j * height + i, step), :] = block[:, j * LANES : (j + 1) * LANES]
    return at + height * right_ref.shape[1] // LANES


def small_rows(position, small, small_got):
    width = small.shape[1]
    mask_at = 3 * width // 4
    rows = []
    for i in range(4):
        for j in range(0, width, LANES):
            row = small[i : i + 1, j : j + LANES]
            if i == 2 and j >= mask_at:
                row = jnp.where(position[0] == 0, row, small_got[i : i + 1, j : j + LANES])
            rows.append(row)
    return jnp.concatenate(rows, axis=0).astype(BF16)


def wgrad_kernel(products, with_small, position, *refs):
    *ins, keep_ref, send_ref, full = refs
    at = 0
    for i in range(products):
        at = blocked_product(ins[2 * i], ins[2 * i + 1], full, at)
    if with_small:
        rows = small_rows(position, *ins[2 * products :])
        full[pl.ds(at, rows.shape[0]), :] = rows
        at += rows.shape[0]
    if at < full.shape[0]:
        full[pl.ds(at, full.shape[0] - at), :] = jnp.zeros((full.shape[0] - at, LANES), BF16)
    half = full.shape[0] // 2
    bit = position[2]
    keep_ref[...] = full[pl.ds(pl.multiple_of(bit * half, 16), half), :]
    send_ref[...] = full[pl.ds(pl.multiple_of((1 - bit) * half, 16), half), :]


def split_kernel(step, position, keep, got, keep_ref, send_ref):
    half = keep_ref.shape[0]
    bit = position[2 + step]
    for at, out in ((bit * half, keep_ref), ((1 - bit) * half, send_ref)):
        rows = pl.ds(pl.multiple_of(at, 16), half)
        out[...] = (keep[rows, :].astype(F32) + got[rows, :].astype(F32)).astype(BF16)


def add_kernel(keep, got, out):
    out[...] = (keep[...].astype(F32) + got[...].astype(F32)).astype(BF16)


def join_kernel(step, position, mine, got, out):
    half = mine.shape[0]
    bit = position[2 + step]
    out[pl.ds(pl.multiple_of(bit * half, 16), half), :] = mine[...]
    out[pl.ds(pl.multiple_of((1 - bit) * half, 16), half), :] = got[...]


def finish_kernel(blocks, cuts, step, position, mine, got, *refs):
    *outs, full = refs
    join_kernel(step, position, mine, got, full)
    at = 0
    for out in outs[:blocks]:
        _, rows, cols = out.shape
        for j in range(cols // LANES):
            out[0, :, pl.ds(j * LANES, LANES)] = full[pl.ds(at, rows), :].astype(F32)
            at += rows
    if cuts:
        small = full[pl.ds(at, sum(cuts)), :].astype(F32)
        at = 0
        for out, count in zip(outs[blocks:], cuts):
            width = out.shape[-1]
            for k in range(count):
                row, col = divmod(k * LANES, width)
                piece = small[at + k : at + k + 1]
                if len(out.shape) == 3:
                    out[0, pl.ds(row, 1), pl.ds(col, LANES)] = piece
                else:
                    out[:, pl.ds(col, LANES)] = piece
            at += count


def call(kernel, outs, position, args, scratch=(), name=None, flops=10**6):
    whole = pl.BlockSpec(memory_space=pltpu.VMEM)
    first = [] if position is None else [position]
    return pl.pallas_call(
        kernel,
        out_shape=outs,
        in_specs=[pl.BlockSpec(memory_space=pltpu.SMEM)] * len(first) + [whole] * len(args),
        out_specs=[whole] * len(outs),
        scratch_shapes=list(scratch),
        compiler_params=pltpu.CompilerParams(vmem_limit_bytes=VMEM_LIMIT),
        cost_estimate=pl.CostEstimate(flops=flops, bytes_accessed=10**5, transcendentals=0),
        name=name,
    )(*first, *[vmem(a) for a in args])


def reduce_steps(n):
    steps = [(1 << b, 1 << b) for b in range(n.bit_length() - 1)]
    if len(steps) >= 3:
        steps[1], steps[2] = (2, 4), (4, 2)
    return steps


def swap(x, masks, n):
    return lax.ppermute(x, "dp", [(i, i ^ masks[i & 1]) for i in range(n)])


def upper(me, masks):
    mask = jnp.where(me & 1, masks[1], masks[0])
    return ((me & mask) != 0).astype(jnp.int32)


def group_sums(groups, position, n, aside):
    steps = reduce_steps(n)
    last = len(steps) - 1
    state = []
    for name, products, extra, shapes, small_shapes in groups:
        height = sum(math.prod(s) for s in shapes + small_shapes) // LANES
        height = -(-height // (8 * n)) * 8 * n
        half = pltpu.VMEM((height // 2, LANES), BF16)
        flat = [x for pair in products for x in pair] + list(extra)
        work = sum(2 * l.shape[0] * l.shape[1] * r.shape[1] for l, r in products)
        keep, send = call(
            functools.partial(wgrad_kernel, len(products), bool(extra)),
            [half, half],
            position,
            flat,
            [pltpu.VMEM((height, LANES), BF16)],
            "wgrad_" + name,
            work,
        )
        keep, position = lax.optimization_barrier((keep, position))
        state.append((keep, send))
    results = [None] * len(groups)
    total = 2 * last + 1
    for t in range(total + len(groups) - 1):
        for g, (name, _, _, shapes, small_shapes) in enumerate(groups):
            s = t - g
            if not 0 <= s < total:
                continue
            keep, send = state[g]
            if s < last:
                got = swap(send, steps[s], n)
                if s + 1 < last:
                    half = pltpu.VMEM((keep.shape[0] // 2, LANES), BF16)
                    state[g] = call(
                        functools.partial(split_kernel, s + 1), [half, half], position, [keep, got], name="split"
                    )
                else:
                    (both,) = call(add_kernel, [pltpu.VMEM(keep.shape, BF16)], None, [keep, got], name="add")
                    state[g] = (both, both)
            elif s == last:
                got = swap(send, steps[last], n)
                (both,) = call(add_kernel, [pltpu.VMEM(keep.shape, BF16)], None, [keep, got], name="add")
                if g == 0:
                    both, aside = lax.optimization_barrier((both, aside))
                state[g] = (both, both)
            else:
                step = 2 * last - s
                got = swap(send, steps[step], n)
                if step > 0:
                    out = pltpu.VMEM((2 * keep.shape[0], LANES), BF16)
                    (both,) = call(
                        functools.partial(join_kernel, step), [out], position, [keep, got], name="join"
                    )
                    state[g] = (both, both)
                else:
                    results[g] = call(
                        functools.partial(
                            finish_kernel, len(shapes), [math.prod(s) // LANES for s in small_shapes], step
                        ),
                        [jax.ShapeDtypeStruct(s, F32) for s in shapes + small_shapes],
                        position,
                        [keep, got],
                        [pltpu.VMEM((2 * keep.shape[0], LANES), BF16)],
                        "finish_" + name,
                    )
    return results, aside


def shards(
    tokens,
    mask_emb,
    mask_idx,
    centers,
    cotangent,
    ln_gain,
    ln_bias,
    qkv_w,
    proj_w,
    out_bias,
    fc1_w,
    fc1_b,
    fc2_w,
    pos_w1,
    pos_b1,
    pos_w2,
    pos_b2,
):
    M, C, rows_in, D = tokens.shape
    FF = fc1_w.shape[2]
    PR = -(-rows_in // 8) * 8
    R = C * PR
    total = M * R
    role = lax.axis_index("section")
    clouds = M * C
    base_args = [
        tokens.reshape(clouds, rows_in, D),
        mask_emb.reshape(1, D),
        mask_idx.reshape(clouds, -1),
        centers.reshape(3, clouds, -1),
        cotangent.reshape(clouds, rows_in, D),
        ln_gain[0],
        ln_bias[0],
        qkv_w[0],
        proj_w[0],
        out_bias[0],
        fc1_w[0],
        fc1_b.reshape(1, FF),
        fc2_w[0],
        pos_w1[0],
        pos_b1.reshape(1, -1),
        pos_w2[0],
        pos_b2.reshape(1, D),
    ]
    base_args = [vmem(a) for a in base_args]
    buf_shapes = [((total, w * LANES), dt) for _, w, dt in SAVES]
    buf_shapes += [
        ((clouds * HEADS * PR, PR), BF16),
        ((total, 1), F32),
        ((total, 1), F32),
        ((total, D), F32),
        ((8, FF), F32),
    ]
    cfg = (C, rows_in, PR, D, FF)
    whole = pl.BlockSpec(memory_space=pltpu.VMEM)
    n_dp = lax.axis_size("dp")
    me = lax.axis_index("dp")
    position = jnp.stack([role, me] + [upper(me, masks) for masks in reduce_steps(n_dp)]).astype(jnp.int32)
    chunks, at = [], 0
    for count in tick_units(M):
        chunks.append((at, count))
        at += count
    *bufs, blank = pl.pallas_call(
        alloc_kernel,
        out_shape=[pltpu.VMEM(s, d) for s, d in buf_shapes + [((R, D), BF16)]],
        in_specs=[pl.BlockSpec(memory_space=pltpu.SMEM)] + [whole] * len(base_args),
        out_specs=[whole] * (len(buf_shapes) + 1),
        compiler_params=pltpu.CompilerParams(vmem_limit_bytes=VMEM_LIMIT),
        name="alloc",
    )(position, *base_args)

    def tick(t, bufs, recv, send_units):
        args = [position] + base_args + [vmem(recv)] + [vmem(b) for b in bufs]
        n_in = len(args)
        outs = pl.pallas_call(
            functools.partial(tick_kernel, cfg, tick_plan(chunks, t, M)),
            out_shape=[pltpu.VMEM(s, d) for s, d in buf_shapes + [((send_units * R, D), BF16)]],
            in_specs=[pl.BlockSpec(memory_space=pltpu.SMEM)] + [whole] * (n_in - 1),
            out_specs=[whole] * (len(buf_shapes) + 1),
            scratch_shapes=tick_scratch(cfg),
            input_output_aliases={n_in - len(bufs) + i: i for i in range(len(bufs))},
            compiler_params=pltpu.CompilerParams(vmem_limit_bytes=VMEM_LIMIT),
            cost_estimate=pl.CostEstimate(flops=4 * 10**9, bytes_accessed=10**6, transcendentals=0),
            name=f"tick{t}",
        )(*args)
        return list(outs[:-1]), outs[-1]

    sections = lax.axis_size("section")
    swap_sections = [(i, sections - 1 - i) for i in range(sections)]
    sent = []
    last_tick = len(chunks) + 2 * LAG - 1
    for t in range(last_tick + 1):
        recv = lax.ppermute(sent[t - LAG], "section", swap_sections) if t >= LAG else blank
        counts = [chunks[i][1] for i in (t, t - LAG) if 0 <= i < len(chunks)]
        bufs, send = tick(t, bufs, recv, max(counts, default=1))
        sent.append(send)
    b = dict(zip([s[0] for s in SAVES] + ["p", "rs1", "rs2", "dx", "small"], bufs, strict=True))

    small_got = lax.ppermute(b["small"], "section", swap_sections)
    groups = [
        ("fc2", [(b["u"], b["dyb"])], (), [(1, FF, D)], []),
        ("fc1", [(b["n2"], b["gu"])], (), [(1, D, FF)], []),
        (
            "rest",
            [(b["n1"], b["qkv"]), (b["o"], b["vh2"]), (b["pc"], b["vh1"])],
            (b["small"], small_got),
            [(1, D, 3 * D), (1, D, D), (1, LANES, D)],
            [(1, FF), (1, 2, D), (1, 2, D), (1, 2, D), (1, D), (1, D), (1, 3, LANES), (1, LANES), (1, FF - 4 * LANES)],
        ),
    ]
    section_out = b["yb"].reshape(M, C, PR, D)[None, :, :, :rows_in]
    section_grad = b["dx"].reshape(M, C, PR, D)[None, :, :, :rows_in]
    sums, (section_out, section_grad) = group_sums(groups, position, n_dp, (section_out, section_grad))
    (fc2_g,), (fc1_g,), rest = sums
    qkv_g, proj_g, pos_g, fc1_b_g, gain_g, bias_g, ob_g, pb2_g, mask_g, pw1_g, pb1_g, _ = rest
    return (
        section_out,
        section_grad,
        mask_g[0],
        gain_g,
        bias_g,
        qkv_g,
        proj_g,
        ob_g,
        fc1_g,
        fc1_b_g,
        fc2_g,
        pw1_g,
        pb1_g,
        pos_g,
        pb2_g,
    )


def solution(mesh):
    return jax.shard_map(
        shards,
        mesh=mesh,
        in_specs=(
            P(None, "dp", None, None),
            P(),
            P(None, "dp", None),
            P(None, None, "dp", None),
            P(None, "dp", None, None),
            P("section", None, None),
            P("section", None, None),
            P("section", None, None),
            P("section", None, None),
            P("section", None, None),
            P("section", None, None),
            P("section", None),
            P("section", None, None),
            P("section", None, None),
            P("section", None),
            P("section", None, None),
            P("section", None),
        ),
        out_specs=(
            P("section", None, "dp", None, None),
            P("section", None, "dp", None, None),
            P(),
            P("section", None, None),
            P("section", None, None),
            P("section", None, None),
            P("section", None, None),
            P("section", None, None),
            P("section", None, None),
            P("section", None),
            P("section", None, None),
            P("section", None, None),
            P("section", None),
            P("section", None, None),
            P("section", None),
        ),
        check_vma=False,
    )
```

```python
import functools
import math

import jax
import jax.numpy as jnp
from jax import lax
from jax.experimental import pallas as pl
from jax.experimental.pallas import tpu as pltpu
from jax.sharding import PartitionSpec as P

HEADS = 6
HD = 64
EPS = 1e-05
LANES = 128
MIB = 1 << 20
TICK_UNITS = (1, 1, 1, 1, 1, 1)
LAG = 2
QKV_COLS = 768
HID = 256
SUB = 288
HALF = 288
GW = 1536
GQ = 768
PHASES = True
VMEM_LIMIT = 12 * MIB

F32 = jnp.float32
BF16 = jnp.bfloat16

ERF_P = 0.375
ERF_C = (
    0.21137403,
    0.21522517,
    0.16911028,
    0.27655959,
    -0.12036233,
    0.3812622,
    -0.1331683,
)
ROOT_HALF = 0.7071067811865476
HALF_LOG2_E = -0.7213475204444817
INV_ROOT_TWO_PI = 0.3989422804014327


def gelu_pair(f):
    den = 1.0 + (ERF_P * ROOT_HALF) * jnp.abs(f)
    t = pl.reciprocal(den, approx=True)
    e = jnp.exp2((f * f) * HALF_LOG2_E)
    poly = 0.5 * ERF_C[-1]
    for c in ERF_C[-2::-1]:
        poly = poly * t + 0.5 * c
    q = e * (t * poly)
    cdf = jnp.where(f >= 0, 1.0 - q, q)
    return f * cdf, cdf + f * (INV_ROOT_TWO_PI * e)


def dot(a, b):
    return jnp.dot(a, b, preferred_element_type=F32)


def dot_t(a, b):
    return lax.dot_general(a, b, (((1,), (1,)), ((), ())), preferred_element_type=F32)


def dot_c(a, b):
    return lax.dot_general(a, b, (((0,), (0,)), ((), ())), preferred_element_type=F32)


def dot_c_f32(a, b):
    return lax.dot_general(
        a, b, (((0,), (0,)), ((), ())), preferred_element_type=F32, precision=lax.Precision.HIGHEST
    )


def dot_f32(a, b):
    return jnp.dot(a, b, preferred_element_type=F32, precision=lax.Precision.HIGHEST)


def centre_rows(centers_ref, cloud):
    patch_count = centers_ref.shape[2]
    rows = [centers_ref[i, pl.ds(cloud, 1), :] for i in range(3)]
    body = jnp.concatenate(rows, axis=0)
    body = jnp.concatenate([jnp.zeros((3, 1), F32), body], axis=1)
    body = jnp.concatenate([body, jnp.zeros((3, LANES - 1 - patch_count), F32)], axis=1)
    return jnp.concatenate([body, jnp.ones((1, LANES), F32), jnp.zeros((4, LANES), F32)], axis=0)


def masked_rows(mask_idx_ref, cloud, padded):
    ids = mask_idx_ref[pl.ds(cloud, 1), :]
    rows = lax.broadcasted_iota(jnp.int32, (padded, ids.shape[1]), 0) - 1
    return jnp.max((rows == ids).astype(F32), axis=1, keepdims=True) > 0.0


def norm_stats(v):
    width = v.shape[1]
    mean = jnp.sum(v, axis=1, keepdims=True) * (1.0 / width)
    cen = v - mean
    var = jnp.sum(cen * cen, axis=1, keepdims=True) * (1.0 / width)
    rs = lax.rsqrt(var + EPS)
    return cen * rs, rs


def norm_back(dn, gain, vhat, rs):
    width = dn.shape[1]
    dg = dn * gain
    m1 = jnp.sum(dg, axis=1, keepdims=True) * (1.0 / width)
    m2 = jnp.sum(dg * vhat, axis=1, keepdims=True) * (1.0 / width)
    return rs * (dg - m1 - vhat * m2)


def colsum(v):
    return jnp.sum(v, axis=0, keepdims=True)


def stack_heads(pair, low):
    zero = jnp.zeros_like(pair)
    return jnp.concatenate([jnp.where(low, pair, zero), jnp.where(low, zero, pair)], axis=0)


def merge_heads(stacked, low):
    n = stacked.shape[0] // 2
    return jnp.where(low, stacked[:n], stacked[n:])


SAVES = (
    ("pc", 1, BF16),
    ("gz", 1, BF16),
    ("vh1", 3, BF16),
    ("n1", 3, BF16),
    ("qkv", 9, BF16),
    ("o", 3, BF16),
    ("vh2", 3, BF16),
    ("n2", 3, BF16),
    ("u", 12, BF16),
    ("gu", 12, BF16),
    ("dyb", 3, BF16),
    ("yb", 3, BF16),
)


def alloc_kernel(count, *refs):
    sources, targets, sem = refs[:count], refs[count : 2 * count], refs[-1]
    copies = [
        pltpu.make_async_copy(source, target, sem.at[i])
        for i, (source, target) in enumerate(zip(sources, targets, strict=True))
    ]
    for copy in copies:
        copy.start()
    for ref in refs[-3:-1]:
        ref[...] = jnp.zeros(ref.shape, ref.dtype)
    for copy in copies:
        copy.wait()


def tick_kernel(cfg, plan, *refs):
    (C, rows_in, PR, D, FF) = cfg
    R = C * PR
    names = ["position", "tokens", "memb", "mask_idx", "centers", "cot"]
    names += ["gain", "bias", "qkv_w", "proj_w", "ob", "fc1_w", "fc1_b", "fc2_w", "pw1", "pb1", "pw2", "pb2"]
    names += ["recv"]
    buf_names = [s[0] for s in SAVES] + ["p", "rs1", "rs2", "dx", "small"]
    names += ["old_" + b for b in buf_names]
    names += buf_names + ["send"]
    scratch_names = ["X", "H", "Q", "O", "G", "S", "FA", "FB"]
    names += scratch_names
    r = dict(zip(names, refs, strict=True))
    role = r["position"][0]
    first = role == 0
    pairs = HEADS // 2
    low = lax.broadcasted_iota(jnp.int32, (PR, LANES), 1) < HD
    scale = HD**-0.5
    X, H, Q, O, G, S, FA, FB = (r[s] for s in scratch_names)
    small = r["small"]
    units = [(c, j) for c in range(C) for j in range(pairs)]
    chunks = FF // HID

    def run(which, body):
        (from0, count0), (from1, count1) = plan[0][which], plan[1][which]
        if count0 == count1 == 0:
            return
        start = jnp.where(first, from0, from1)
        count = jnp.where(first, count0, count1)

        def step(k, carry):
            body(start + k, k)
            return carry

        lax.fori_loop(0, count, step, 0)

    def rows_of(c):
        return pl.ds(c * PR, PR)

    def unit_rows(unit, i):
        return pl.ds(pl.multiple_of((unit * C * pairs + i) * 2 * PR, 16), 2 * PR)

    def scores(i):
        return pl.ds(i * 2 * PR, 2 * PR)

    def cols(j):
        return pl.ds(j * HID, HID)

    def staged(stages, count):
        for i in range(count + len(stages) - 1):
            for lag, stage in enumerate(stages):
                if 0 <= i - lag < count:
                    stage(i - lag)

    def position(unit, k):
        here = pl.ds(pl.multiple_of(unit * R, 16), R)
        w1 = jnp.concatenate([r["pw1"][i] for i in range(3)] + [r["pb1"][...], jnp.zeros((4, LANES), F32)], axis=0)
        for c in range(C):
            O[rows_of(c), :LANES] = dot_c_f32(centre_rows(r["centers"], unit * C + c), w1)[:PR]
        pc, gz = gelu_pair(O[:, :LANES])
        r["pc"][here, :] = pc.astype(BF16)
        r["gz"][here, :] = gz.astype(BF16)

    def forward(unit, k):
        base = pl.multiple_of(unit * R, 16)
        cloud0 = unit * C
        here = pl.ds(base, R)
        mail = pl.ds(pl.multiple_of(k * R, 16), R)

        def saved(at, count):
            return pl.ds(pl.multiple_of(base + at, 16), count)

        @pl.when(first)
        def _():
            X[...] = jnp.zeros(X.shape, F32)
            memb = r["memb"][...].astype(F32)
            for c in range(C):
                hit = masked_rows(r["mask_idx"], cloud0 + c, PR)[:rows_in]
                tok = r["tokens"][cloud0 + c].astype(F32)
                X[pl.ds(c * PR, rows_in), :] = jnp.where(hit, memb, tok)

        @pl.when(role != 0)
        def _():
            X[...] = r["recv"][mail, :].astype(F32)

        H[...] = X[...] + dot(r["pc"][here, :], r["pw2"][...]) + r["pb2"][...]
        for at in range(0, R, SUB):
            vh1, rs1 = norm_stats(H[pl.ds(at, SUB), :])
            r["rs1"][saved(at, SUB), :] = rs1
            r["vh1"][saved(at, SUB), :] = vh1.astype(BF16)
            r["n1"][saved(at, SUB), :] = (vh1 * r["gain"][0:1] + r["bias"][0:1]).astype(BF16)
        for at in range(0, 3 * D, QKV_COLS):
            col = pl.ds(at, min(QKV_COLS, 3 * D - at))
            qkv = dot(r["n1"][here, :], r["qkv_w"][:, col]).astype(BF16)
            r["qkv"][here, col] = qkv
            Q[:, col] = qkv.astype(F32)
        key_ok = lax.broadcasted_iota(jnp.int32, (2 * PR, PR), 1) < rows_in

        def score(i):
            c, j = units[i]
            q = Q[rows_of(c), pl.ds(j * LANES, LANES)] * scale
            k = Q[rows_of(c), pl.ds(D + j * LANES, LANES)].astype(BF16)
            S[scores(i), :] = dot_t(stack_heads(q, low).astype(BF16), k)

        def soften(i):
            s = jnp.where(key_ok, S[scores(i), :], -1e30)
            e = jnp.exp(s - jnp.max(s, axis=1, keepdims=True))
            p = (e * pl.reciprocal(jnp.sum(e, axis=1, keepdims=True))).astype(BF16)
            r["p"][unit_rows(unit, i), :] = p

        def weigh(i):
            c, j = units[i]
            v = Q[rows_of(c), pl.ds(2 * D + j * LANES, LANES)].astype(BF16)
            o = merge_heads(dot(r["p"][unit_rows(unit, i), :], v), low)
            O[rows_of(c), pl.ds(j * LANES, LANES)] = o

        if PHASES:
            for stage in (score, soften, weigh):
                staged([stage], len(units))
        else:
            staged([score, soften, weigh], len(units))
        o = O[...].astype(BF16)
        r["o"][here, :] = o
        H[...] += dot(o, r["proj_w"][...]) + r["ob"][0:1]
        for at in range(0, R, SUB):
            res = H[pl.ds(at, SUB), :]
            vh2, rs2 = norm_stats(res)
            r["rs2"][saved(at, SUB), :] = rs2
            r["vh2"][saved(at, SUB), :] = vh2.astype(BF16)
            r["n2"][saved(at, SUB), :] = (vh2 * r["gain"][1:2] + r["bias"][1:2]).astype(BF16)
            H[pl.ds(at, SUB), :] = res + r["ob"][1:2]

        def enter(i):
            j, part = divmod(i, R // HALF)
            buf = (FA, FB)[j % 2]
            n2 = r["n2"][saved(part * HALF, HALF), :]
            buf[pl.ds(part * HALF, HALF), :] = dot(n2, r["fc1_w"][:, cols(j)]) + r["fc1_b"][:, cols(j)]

        def leave(i):
            j, part = divmod(i, R // HALF)
            buf = (FA, FB)[j % 2]
            for at in range(part * HALF, (part + 1) * HALF, SUB):
                u, gu = gelu_pair(buf[pl.ds(at, SUB), :])
                r["u"][saved(at, SUB), cols(j)] = u.astype(BF16)
                r["gu"][saved(at, SUB), cols(j)] = gu.astype(BF16)

        def close(i):
            j, part = divmod(i, R // HALF)
            H[pl.ds(part * HALF, HALF), :] += dot(r["u"][saved(part * HALF, HALF), cols(j)], r["fc2_w"][cols(j), :])

        staged([enter, leave, close], chunks * R // HALF)
        y = H[...].astype(BF16)
        r["yb"][here, :] = y

        @pl.when(first)
        def _():
            r["send"][mail, :] = y

    def backward(unit, k):
        base = pl.multiple_of(unit * R, 16)
        cloud0 = unit * C
        here = pl.ds(base, R)
        mail = pl.ds(pl.multiple_of(k * R, 16), R)

        def saved(at, count):
            return pl.ds(pl.multiple_of(base + at, 16), count)

        @pl.when(role != 0)
        def _():
            X[...] = jnp.zeros(X.shape, F32)
            for c in range(C):
                X[pl.ds(c * PR, rows_in), :] = r["cot"][cloud0 + c].astype(F32)

        @pl.when(first)
        def _():
            X[...] = r["recv"][mail, :].astype(F32)

        r["dyb"][here, :] = X[...].astype(BF16)
        small[2:3, pl.ds(D, D)] += colsum(X[...])

        for at in range(0, FF, GW):
            col = pl.ds(at, GW)
            df = dot_t(r["dyb"][here, :], r["fc2_w"][col, :]) * r["gu"][here, col].astype(F32)
            small[0:1, col] += colsum(df)
            dfb = df.astype(BF16)
            r["gu"][here, col] = dfb
            part = dot_t(dfb, r["fc1_w"][:, col])
            H[...] = part if at == 0 else H[...] + part
        sums = [0.0] * 3
        for at in range(0, R, SUB):
            rows = pl.ds(at, SUB)
            dn2 = H[rows, :]
            vh2 = r["vh2"][saved(at, SUB), :].astype(F32)
            dr = X[rows, :] + norm_back(dn2, r["gain"][1:2], vh2, r["rs2"][saved(at, SUB), :])
            X[rows, :] = dr
            r["vh2"][saved(at, SUB), :] = dr.astype(BF16)
            sums = [s + colsum(v) for s, v in zip(sums, (dn2 * vh2, dn2, dr))]
        for row, at, s in zip((1, 1, 2), (D, 3 * D, 0), sums):
            small[row : row + 1, pl.ds(at, D)] += s
        G[...] = dot_t(r["vh2"][here, :], r["proj_w"][...]).astype(BF16).astype(F32)
        Q[...] = r["qkv"][here, :].astype(F32)

        def do_of(i):
            c, j = units[i]
            return stack_heads(G[rows_of(c), pl.ds(j * LANES, LANES)], low).astype(BF16)

        def score(i):
            c, j = units[i]
            v = Q[rows_of(c), pl.ds(2 * D + j * LANES, LANES)].astype(BF16)
            S[scores(i), :] = dot_t(do_of(i), v)

        def soften(i):
            p = r["p"][unit_rows(unit, i), :].astype(F32)
            dp = S[scores(i), :]
            ds = p * (dp - jnp.sum(dp * p, axis=1, keepdims=True))
            S[scores(i), :] = ds * scale

        def weigh(i):
            c, j = units[i]
            at = rows_of(c)
            q_at, k_at, v_at = (pl.ds(m * D + j * LANES, LANES) for m in range(3))
            q = stack_heads(Q[at, q_at], low).astype(BF16)
            k = Q[at, k_at].astype(BF16)
            dsb = S[scores(i), :].astype(BF16)
            dq = merge_heads(dot(dsb, k), low)
            dk = dot_c(dsb, q)
            Q[at, v_at] = dot_c(r["p"][unit_rows(unit, i), :], do_of(i))
            Q[at, q_at] = dq
            Q[at, k_at] = dk

        if PHASES:
            for stage in (score, soften, weigh):
                staged([stage], len(units))
        else:
            staged([score, soften, weigh], len(units))
        for at in range(0, 3 * D, GQ):
            col = pl.ds(at, min(GQ, 3 * D - at))
            dqkv = Q[:, col].astype(BF16)
            r["qkv"][here, col] = dqkv
            part = dot_t(dqkv, r["qkv_w"][:, col])
            H[...] = part if at == 0 else H[...] + part
        sums = [0.0] * 3
        for at in range(0, R, SUB):
            rows = pl.ds(at, SUB)
            dn1 = H[rows, :]
            vh1 = r["vh1"][saved(at, SUB), :].astype(F32)
            dh = X[rows, :] + norm_back(dn1, r["gain"][0:1], vh1, r["rs1"][saved(at, SUB), :])
            X[rows, :] = dh
            r["vh1"][saved(at, SUB), :] = dh.astype(BF16)
            sums = [s + colsum(v) for s, v in zip(sums, (dn1 * vh1, dn1, dh))]
        for row, at, s in zip((1, 1, 2), (0, 2 * D, 2 * D), sums):
            small[row : row + 1, pl.ds(at, D)] += s
        dhb = r["vh1"][here, :]

        @pl.when(role != 0)
        def _():
            r["send"][mail, :] = dhb

        O[:, :LANES] = dot_t(dhb, r["pw2"][...]) * r["gz"][here, :].astype(F32)
        for c in range(C):
            cen = centre_rows(r["centers"], cloud0 + c)
            dz = jnp.concatenate([O[rows_of(c), :LANES], jnp.zeros((LANES - PR, LANES), F32)], axis=0)
            dw = dot_f32(cen, dz)
            for i in range(4):
                small[3:4, pl.ds(i * LANES, LANES)] += dw[i : i + 1]
            dx_at = pl.ds(pl.multiple_of(base + c * PR, 8), PR)

            @pl.when(first)
            def _():
                hit = masked_rows(r["mask_idx"], cloud0 + c, PR)
                dx = X[rows_of(c), :]
                r["dx"][dx_at, :] = jnp.where(hit, 0.0, dx)
                small[2:3, pl.ds(3 * D, D)] += colsum(jnp.where(hit, dx, 0.0))

            @pl.when(role != 0)
            def _():
                r["dx"][dx_at, :] = X[rows_of(c), :]

    run(0, position)
    run(1, forward)
    run(2, backward)


def tick_units(units):
    if sum(TICK_UNITS) == units:
        return TICK_UNITS
    return (1,) * units


def tick_plan(chunks, t, units):
    none = (0, 0)

    def chunk(i):
        return chunks[i] if 0 <= i < len(chunks) else none

    half = -(-units // LAG)
    early = (t * half, min(half, units - t * half)) if t < LAG else none
    return (chunk(t), chunk(t), chunk(t - 2 * LAG)), (early, chunk(t - LAG), chunk(t - LAG))


def tick_scratch(cfg):
    (C, _, PR, D, _) = cfg
    R = C * PR
    wide = [(R, D), (R, D), (R, 3 * D), (R, D), (R, D), (C * HEADS * PR, PR), (R, HID), (R, HID)]
    return [pltpu.VMEM(shape, F32) for shape in wide]


def vmem(x):
    return pltpu.with_memory_space_constraint(x, pltpu.VMEM)


def blocked_product(left_ref, right_ref, out_ref, at):
    height = left_ref.shape[1]
    step = min(height, 384)
    for i in range(0, height, step):
        block = dot_c(left_ref[:, pl.ds(i, step)], right_ref[...]).astype(BF16)
        for j in range(right_ref.shape[1] // LANES):
            out_ref[pl.ds(at + j * height + i, step), :] = block[:, j * LANES : (j + 1) * LANES]
    return at + height * right_ref.shape[1] // LANES


def small_rows(position, small, small_got):
    width = small.shape[1]
    mask_at = 3 * width // 4
    rows = []
    for i in range(4):
        for j in range(0, width, LANES):
            row = small[i : i + 1, j : j + LANES]
            if i == 2 and j >= mask_at:
                row = jnp.where(position[0] == 0, row, small_got[i : i + 1, j : j + LANES])
            rows.append(row)
    return jnp.concatenate(rows, axis=0).astype(BF16)


def wgrad_kernel(products, with_small, position, *refs):
    *ins, keep_ref, send_ref, full = refs
    at = 0
    for i in range(products):
        at = blocked_product(ins[2 * i], ins[2 * i + 1], full, at)
    if with_small:
        rows = small_rows(position, *ins[2 * products :])
        full[pl.ds(at, rows.shape[0]), :] = rows
        at += rows.shape[0]
    if at < full.shape[0]:
        full[pl.ds(at, full.shape[0] - at), :] = jnp.zeros((full.shape[0] - at, LANES), BF16)
    half = full.shape[0] // 2
    bit = position[2]
    keep_ref[...] = full[pl.ds(pl.multiple_of(bit * half, 16), half), :]
    send_ref[...] = full[pl.ds(pl.multiple_of((1 - bit) * half, 16), half), :]


def split_kernel(step, position, keep, got, keep_ref, send_ref):
    half = keep_ref.shape[0]
    bit = position[2 + step]
    for at, out in ((bit * half, keep_ref), ((1 - bit) * half, send_ref)):
        rows = pl.ds(pl.multiple_of(at, 16), half)
        out[...] = (keep[rows, :].astype(F32) + got[rows, :].astype(F32)).astype(BF16)


def add_kernel(keep, got, out):
    out[...] = (keep[...].astype(F32) + got[...].astype(F32)).astype(BF16)


def join_kernel(step, position, mine, got, out):
    half = mine.shape[0]
    bit = position[2 + step]
    out[pl.ds(pl.multiple_of(bit * half, 16), half), :] = mine[...]
    out[pl.ds(pl.multiple_of((1 - bit) * half, 16), half), :] = got[...]


def finish_kernel(blocks, cuts, step, position, mine, got, *refs):
    *outs, full = refs
    join_kernel(step, position, mine, got, full)
    at = 0
    for out in outs[:blocks]:
        _, rows, cols = out.shape
        for j in range(cols // LANES):
            out[0, :, pl.ds(j * LANES, LANES)] = full[pl.ds(at, rows), :].astype(F32)
            at += rows
    if cuts:
        small = full[pl.ds(at, sum(cuts)), :].astype(F32)
        at = 0
        for out, count in zip(outs[blocks:], cuts):
            width = out.shape[-1]
            for k in range(count):
                row, col = divmod(k * LANES, width)
                piece = small[at + k : at + k + 1]
                if len(out.shape) == 3:
                    out[row // out.shape[1], pl.ds(row % out.shape[1], 1), pl.ds(col, LANES)] = piece
                else:
                    out[:, pl.ds(col, LANES)] = piece
            at += count


def call(kernel, outs, position, args, scratch=(), name=None, flops=10**6):
    whole = pl.BlockSpec(memory_space=pltpu.VMEM)
    first = [] if position is None else [position]
    return pl.pallas_call(
        kernel,
        out_shape=outs,
        in_specs=[pl.BlockSpec(memory_space=pltpu.SMEM)] * len(first) + [whole] * len(args),
        out_specs=[whole] * len(outs),
        scratch_shapes=list(scratch),
        compiler_params=pltpu.CompilerParams(vmem_limit_bytes=VMEM_LIMIT),
        cost_estimate=pl.CostEstimate(flops=max(flops, 8 * 10**8), bytes_accessed=10**5, transcendentals=0),
        name=name,
    )(*first, *[vmem(a) for a in args])


def reduce_steps(n):
    steps = [(1 << b, 1 << b) for b in range(n.bit_length() - 1)]
    if len(steps) >= 3:
        steps[1], steps[2] = (2, 4), (4, 2)
    return steps


def swap(x, masks, n):
    return lax.ppermute(x, "dp", [(i, i ^ masks[i & 1]) for i in range(n)])


def upper(me, masks):
    mask = jnp.where(me & 1, masks[1], masks[0])
    return ((me & mask) != 0).astype(jnp.int32)


def group_products(group, position, n):
    name, products, extra, shapes, small_shapes = group
    height = sum(math.prod(s) for s in shapes + small_shapes) // LANES
    height = -(-height // (8 * n)) * 8 * n
    half = pltpu.VMEM((height // 2, LANES), BF16)
    flat = [x for pair in products for x in pair] + list(extra)
    work = sum(2 * l.shape[0] * l.shape[1] * r.shape[1] for l, r in products)
    keep, send = call(
        functools.partial(wgrad_kernel, len(products), bool(extra)),
        [half, half],
        position,
        flat,
        [pltpu.VMEM((height, LANES), BF16)],
        "wgrad_" + name,
        work,
    )
    keep, position = lax.optimization_barrier((keep, position))
    return (keep, send), position


def group_sums(groups, state, position, n, aside):
    steps = reduce_steps(n)
    last = len(steps) - 1
    results = [None] * len(groups)
    total = 2 * last + 1
    for t in range(total + len(groups) - 1):
        for g, (name, _, _, shapes, small_shapes) in enumerate(groups):
            s = t - g
            if not 0 <= s < total:
                continue
            keep, send = state[g]
            if s < last:
                got = swap(send, steps[s], n)
                if s + 1 < last:
                    half = pltpu.VMEM((keep.shape[0] // 2, LANES), BF16)
                    state[g] = call(
                        functools.partial(split_kernel, s + 1), [half, half], position, [keep, got], name="split"
                    )
                else:
                    (both,) = call(add_kernel, [pltpu.VMEM(keep.shape, BF16)], None, [keep, got], name="add")
                    state[g] = (both, both)
            elif s == last:
                got = swap(send, steps[last], n)
                (both,) = call(add_kernel, [pltpu.VMEM(keep.shape, BF16)], None, [keep, got], name="add")
                if g == 0:
                    both, aside = lax.optimization_barrier((both, aside))
                state[g] = (both, both)
            else:
                step = 2 * last - s
                got = swap(send, steps[step], n)
                if step > 0:
                    out = pltpu.VMEM((2 * keep.shape[0], LANES), BF16)
                    (both,) = call(
                        functools.partial(join_kernel, step), [out], position, [keep, got], name="join"
                    )
                    state[g] = (both, both)
                else:
                    results[g] = call(
                        functools.partial(
                            finish_kernel, len(shapes), [math.prod(s) // LANES for s in small_shapes], step
                        ),
                        [jax.ShapeDtypeStruct(s, F32) for s in shapes + small_shapes],
                        position,
                        [keep, got],
                        [pltpu.VMEM((2 * keep.shape[0], LANES), BF16)],
                        "finish_" + name,
                    )
    return results, aside


def shards(
    tokens,
    mask_emb,
    mask_idx,
    centers,
    cotangent,
    ln_gain,
    ln_bias,
    qkv_w,
    proj_w,
    out_bias,
    fc1_w,
    fc1_b,
    fc2_w,
    pos_w1,
    pos_b1,
    pos_w2,
    pos_b2,
):
    M, C, rows_in, D = tokens.shape
    FF = fc1_w.shape[2]
    PR = -(-rows_in // 8) * 8
    R = C * PR
    total = M * R
    role = lax.axis_index("section")
    clouds = M * C
    base_args = [
        tokens.reshape(clouds, rows_in, D),
        mask_emb.reshape(1, D),
        mask_idx.reshape(clouds, -1),
        centers.reshape(3, clouds, -1),
        cotangent.reshape(clouds, rows_in, D),
        ln_gain[0],
        ln_bias[0],
        qkv_w[0],
        proj_w[0],
        out_bias[0],
        fc1_w[0],
        fc1_b.reshape(1, FF),
        fc2_w[0],
        pos_w1.transpose(1, 0, 2),
        pos_b1.reshape(1, -1),
        pos_w2[0],
        pos_b2.reshape(1, D),
    ]
    buf_shapes = [((total, w * LANES), dt) for _, w, dt in SAVES]
    buf_shapes += [
        ((clouds * HEADS * PR, PR), BF16),
        ((total, 1), F32),
        ((total, 1), F32),
        ((total, D), F32),
        ((8, FF), F32),
    ]
    cfg = (C, rows_in, PR, D, FF)
    whole = pl.BlockSpec(memory_space=pltpu.VMEM)
    n_dp = lax.axis_size("dp")
    me = lax.axis_index("dp")
    position = jnp.stack([role, me] + [upper(me, masks) for masks in reduce_steps(n_dp)]).astype(jnp.int32)
    chunks, at = [], 0
    for count in tick_units(M):
        chunks.append((at, count))
        at += count
    made = pl.pallas_call(
        functools.partial(alloc_kernel, len(base_args)),
        out_shape=[pltpu.VMEM(x.shape, x.dtype) for x in base_args]
        + [pltpu.VMEM(s, d) for s, d in buf_shapes + [((R, D), BF16)]],
        in_specs=[pl.BlockSpec(memory_space=pl.ANY)] * len(base_args),
        out_specs=[whole] * (len(base_args) + len(buf_shapes) + 1),
        scratch_shapes=[pltpu.SemaphoreType.DMA((len(base_args),))],
        compiler_params=pltpu.CompilerParams(vmem_limit_bytes=VMEM_LIMIT),
        name="alloc",
    )(*[pltpu.with_memory_space_constraint(x, pltpu.HBM) for x in base_args])
    base_args = [vmem(x) for x in made[: len(base_args)]]
    *bufs, blank = made[len(base_args) :]

    def tick(t, bufs, recv, send_units):
        args = [position] + base_args + [vmem(recv)] + [vmem(b) for b in bufs]
        n_in = len(args)
        outs = pl.pallas_call(
            functools.partial(tick_kernel, cfg, tick_plan(chunks, t, M)),
            out_shape=[pltpu.VMEM(s, d) for s, d in buf_shapes + [((send_units * R, D), BF16)]],
            in_specs=[pl.BlockSpec(memory_space=pltpu.SMEM)] + [whole] * (n_in - 1),
            out_specs=[whole] * (len(buf_shapes) + 1),
            scratch_shapes=tick_scratch(cfg),
            input_output_aliases={n_in - len(bufs) + i: i for i in range(len(bufs))},
            compiler_params=pltpu.CompilerParams(vmem_limit_bytes=VMEM_LIMIT),
            cost_estimate=pl.CostEstimate(flops=4 * 10**9, bytes_accessed=10**6, transcendentals=0),
            name=f"tick{t}",
        )(*args)
        return list(outs[:-1]), outs[-1]

    sections = lax.axis_size("section")
    swap_sections = [(i, sections - 1 - i) for i in range(sections)]
    sent = []
    last_tick = len(chunks) + 2 * LAG - 1
    names = [s[0] for s in SAVES] + ["p", "rs1", "rs2", "dx", "small"]
    for t in range(last_tick + 1):
        recv = lax.ppermute(sent[t - LAG], "section", swap_sections) if t >= LAG else blank
        counts = [chunks[i][1] for i in (t, t - LAG) if 0 <= i < len(chunks)]
        bufs, send = tick(t, bufs, recv, max(counts, default=1))
        sent.append(send)
    b = dict(zip(names, bufs, strict=True))

    small_got = lax.ppermute(b["small"], "section", swap_sections)
    groups = [
        ("fc2", [(b["u"], b["dyb"])], (), [(1, FF, D)], []),
        ("fc1", [(b["n2"], b["gu"])], (), [(1, D, FF)], []),
        (
            "rest",
            [(b["n1"], b["qkv"]), (b["o"], b["vh2"]), (b["pc"], b["vh1"])],
            (b["small"], small_got),
            [(1, D, 3 * D), (1, D, D), (1, LANES, D)],
            [(1, FF), (1, 2, D), (1, 2, D), (1, 2, D), (1, D), (1, D), (3, 1, LANES), (1, LANES), (1, FF - 4 * LANES)],
        ),
    ]
    section_out = b["yb"].reshape(M, C, PR, D)[None, :, :, :rows_in]
    section_grad = b["dx"].reshape(M, C, PR, D)[None, :, :, :rows_in]
    halves = []
    for group in groups:
        half, position = group_products(group, position, n_dp)
        halves.append(half)
    sums, (section_out, section_grad) = group_sums(groups, halves, position, n_dp, (section_out, section_grad))
    (fc2_g,), (fc1_g,), rest = sums
    qkv_g, proj_g, pos_g, fc1_b_g, gain_g, bias_g, ob_g, pb2_g, mask_g, pw1_g, pb1_g, _ = rest
    return (
        section_out,
        section_grad,
        mask_g[0],
        gain_g,
        bias_g,
        qkv_g,
        proj_g,
        ob_g,
        fc1_g,
        fc1_b_g,
        fc2_g,
        pw1_g.transpose(1, 0, 2),
        pb1_g,
        pos_g,
        pb2_g,
    )


def solution(mesh):
    return jax.shard_map(
        shards,
        mesh=mesh,
        in_specs=(
            P(None, "dp", None, None),
            P(),
            P(None, "dp", None),
            P(None, None, "dp", None),
            P(None, "dp", None, None),
            P("section", None, None),
            P("section", None, None),
            P("section", None, None),
            P("section", None, None),
            P("section", None, None),
            P("section", None, None),
            P("section", None),
            P("section", None, None),
            P("section", None, None),
            P("section", None),
            P("section", None, None),
            P("section", None),
        ),
        out_specs=(
            P("section", None, "dp", None, None),
            P("section", None, "dp", None, None),
            P(),
            P("section", None, None),
            P("section", None, None),
            P("section", None, None),
            P("section", None, None),
            P("section", None, None),
            P("section", None, None),
            P("section", None),
            P("section", None, None),
            P("section", None, None),
            P("section", None),
            P("section", None, None),
            P("section", None),
        ),
        check_vma=False,
    )
```

```python
import functools
import math

import jax
import jax.numpy as jnp
from jax import lax
from jax.experimental import pallas as pl
from jax.experimental.pallas import tpu as pltpu
from jax.sharding import PartitionSpec as P

HEADS = 6
HD = 64
EPS = 1e-05
LANES = 128
MIB = 1 << 20
TICK_UNITS = (1, 1, 1, 1, 1, 1)
LAG = 2
QKV_COLS = 768
HID = 256
SUB = 288
HALF = 288
GW = 1536
GQ = 768
PHASES = True
VMEM_LIMIT = 12 * MIB

F32 = jnp.float32
BF16 = jnp.bfloat16

ERF_P = 0.375
ERF_C = (
    0.21137403,
    0.21522517,
    0.16911028,
    0.27655959,
    -0.12036233,
    0.3812622,
    -0.1331683,
)
ROOT_HALF = 0.7071067811865476
HALF_LOG2_E = -0.7213475204444817
INV_ROOT_TWO_PI = 0.3989422804014327


def gelu_pair(f):
    den = 1.0 + (ERF_P * ROOT_HALF) * jnp.abs(f)
    t = pl.reciprocal(den, approx=True)
    e = jnp.exp2((f * f) * HALF_LOG2_E)
    poly = 0.5 * ERF_C[-1]
    for c in ERF_C[-2::-1]:
        poly = poly * t + 0.5 * c
    q = e * (t * poly)
    cdf = jnp.where(f >= 0, 1.0 - q, q)
    return f * cdf, cdf + f * (INV_ROOT_TWO_PI * e)


def dot(a, b):
    return jnp.dot(a, b, preferred_element_type=F32)


def dot_t(a, b):
    return lax.dot_general(a, b, (((1,), (1,)), ((), ())), preferred_element_type=F32)


def dot_c(a, b):
    return lax.dot_general(a, b, (((0,), (0,)), ((), ())), preferred_element_type=F32)


def dot_c_f32(a, b):
    return lax.dot_general(
        a, b, (((0,), (0,)), ((), ())), preferred_element_type=F32, precision=lax.Precision.HIGHEST
    )


def dot_f32(a, b):
    return jnp.dot(a, b, preferred_element_type=F32, precision=lax.Precision.HIGHEST)


def centre_rows(centers_ref, cloud):
    patch_count = centers_ref.shape[2]
    rows = [centers_ref[i, pl.ds(cloud, 1), :] for i in range(3)]
    body = jnp.concatenate(rows, axis=0)
    body = jnp.concatenate([jnp.zeros((3, 1), F32), body], axis=1)
    body = jnp.concatenate([body, jnp.zeros((3, LANES - 1 - patch_count), F32)], axis=1)
    return jnp.concatenate([body, jnp.ones((1, LANES), F32), jnp.zeros((4, LANES), F32)], axis=0)


def masked_rows(mask_idx_ref, cloud, padded):
    ids = mask_idx_ref[pl.ds(cloud, 1), :]
    rows = lax.broadcasted_iota(jnp.int32, (padded, ids.shape[1]), 0) - 1
    return jnp.max((rows == ids).astype(F32), axis=1, keepdims=True) > 0.0


def norm_stats(v):
    width = v.shape[1]
    mean = jnp.sum(v, axis=1, keepdims=True) * (1.0 / width)
    cen = v - mean
    var = jnp.sum(cen * cen, axis=1, keepdims=True) * (1.0 / width)
    rs = lax.rsqrt(var + EPS)
    return cen * rs, rs


def norm_back(dn, gain, vhat, rs):
    width = dn.shape[1]
    dg = dn * gain
    m1 = jnp.sum(dg, axis=1, keepdims=True) * (1.0 / width)
    m2 = jnp.sum(dg * vhat, axis=1, keepdims=True) * (1.0 / width)
    return rs * (dg - m1 - vhat * m2)


def colsum(v):
    return jnp.sum(v, axis=0, keepdims=True)


def stack_heads(pair, low):
    zero = jnp.zeros_like(pair)
    return jnp.concatenate([jnp.where(low, pair, zero), jnp.where(low, zero, pair)], axis=0)


def merge_heads(stacked, low):
    n = stacked.shape[0] // 2
    return jnp.where(low, stacked[:n], stacked[n:])


SAVES = (
    ("pc", 1, BF16),
    ("gz", 1, BF16),
    ("vh1", 3, BF16),
    ("n1", 3, BF16),
    ("qkv", 9, BF16),
    ("o", 3, BF16),
    ("vh2", 3, BF16),
    ("n2", 3, BF16),
    ("u", 12, BF16),
    ("gu", 12, BF16),
    ("dyb", 3, BF16),
    ("yb", 3, BF16),
)


def alloc_kernel(count, *refs):
    sources, targets, sem = refs[:count], refs[count : 2 * count], refs[-1]
    copies = [
        pltpu.make_async_copy(source, target, sem.at[i])
        for i, (source, target) in enumerate(zip(sources, targets, strict=True))
    ]
    for copy in copies:
        copy.start()
    for ref in refs[-3:-1]:
        ref[...] = jnp.zeros(ref.shape, ref.dtype)
    for copy in copies:
        copy.wait()


def tick_kernel(cfg, plan, *refs):
    (C, rows_in, PR, D, FF) = cfg
    R = C * PR
    names = ["position", "tokens", "memb", "mask_idx", "centers", "cot"]
    names += ["gain", "bias", "qkv_w", "proj_w", "ob", "fc1_w", "fc1_b", "fc2_w", "pw1", "pb1", "pw2", "pb2"]
    names += ["recv"]
    buf_names = [s[0] for s in SAVES] + ["p", "rs1", "rs2", "dx", "small"]
    names += ["old_" + b for b in buf_names]
    names += buf_names + ["send"]
    scratch_names = ["X", "H", "Q", "O", "G", "S", "FA", "FB"]
    names += scratch_names
    r = dict(zip(names, refs, strict=True))
    role = r["position"][0]
    first = role == 0
    pairs = HEADS // 2
    low = lax.broadcasted_iota(jnp.int32, (PR, LANES), 1) < HD
    scale = HD**-0.5
    X, H, Q, O, G, S, FA, FB = (r[s] for s in scratch_names)
    small = r["small"]
    units = [(c, j) for c in range(C) for j in range(pairs)]
    chunks = FF // HID

    def run(which, body):
        (from0, count0), (from1, count1) = plan[0][which], plan[1][which]
        if count0 == count1 == 0:
            return
        start = jnp.where(first, from0, from1)
        count = jnp.where(first, count0, count1)

        def step(k, carry):
            body(start + k, k)
            return carry

        lax.fori_loop(0, count, step, 0)

    def rows_of(c):
        return pl.ds(c * PR, PR)

    def unit_rows(unit, i):
        return pl.ds(pl.multiple_of((unit * C * pairs + i) * 2 * PR, 16), 2 * PR)

    def scores(i):
        return pl.ds(i * 2 * PR, 2 * PR)

    def cols(j):
        return pl.ds(j * HID, HID)

    def staged(stages, count):
        for i in range(count + len(stages) - 1):
            for lag, stage in enumerate(stages):
                if 0 <= i - lag < count:
                    stage(i - lag)

    def position(unit, k):
        here = pl.ds(pl.multiple_of(unit * R, 16), R)
        w1 = jnp.concatenate([r["pw1"][i] for i in range(3)] + [r["pb1"][...], jnp.zeros((4, LANES), F32)], axis=0)
        for c in range(C):
            O[rows_of(c), :LANES] = dot_c_f32(centre_rows(r["centers"], unit * C + c), w1)[:PR]
        pc, gz = gelu_pair(O[:, :LANES])
        r["pc"][here, :] = pc.astype(BF16)
        r["gz"][here, :] = gz.astype(BF16)

    def forward(unit, k):
        base = pl.multiple_of(unit * R, 16)
        cloud0 = unit * C
        here = pl.ds(base, R)
        mail = pl.ds(pl.multiple_of(k * R, 16), R)

        def saved(at, count):
            return pl.ds(pl.multiple_of(base + at, 16), count)

        @pl.when(first)
        def _():
            X[...] = jnp.zeros(X.shape, F32)
            memb = r["memb"][...].astype(F32).reshape(1, D)
            for c in range(C):
                hit = masked_rows(r["mask_idx"], cloud0 + c, PR)[:rows_in]
                tok = r["tokens"][cloud0 + c].astype(F32)
                X[pl.ds(c * PR, rows_in), :] = jnp.where(hit, memb, tok)

        @pl.when(role != 0)
        def _():
            X[...] = r["recv"][mail, :].astype(F32)

        H[...] = X[...] + dot(r["pc"][here, :], r["pw2"][...]) + r["pb2"][...]
        for at in range(0, R, SUB):
            vh1, rs1 = norm_stats(H[pl.ds(at, SUB), :])
            r["rs1"][saved(at, SUB), :] = rs1
            r["vh1"][saved(at, SUB), :] = vh1.astype(BF16)
            r["n1"][saved(at, SUB), :] = (vh1 * r["gain"][0:1] + r["bias"][0:1]).astype(BF16)
        for at in range(0, 3 * D, QKV_COLS):
            col = pl.ds(at, min(QKV_COLS, 3 * D - at))
            qkv = dot(r["n1"][here, :], r["qkv_w"][:, col]).astype(BF16)
            r["qkv"][here, col] = qkv
            Q[:, col] = qkv.astype(F32)
        key_ok = lax.broadcasted_iota(jnp.int32, (2 * PR, PR), 1) < rows_in

        def score(i):
            c, j = units[i]
            q = Q[rows_of(c), pl.ds(j * LANES, LANES)] * scale
            k = Q[rows_of(c), pl.ds(D + j * LANES, LANES)].astype(BF16)
            S[scores(i), :] = dot_t(stack_heads(q, low).astype(BF16), k)

        def soften(i):
            s = jnp.where(key_ok, S[scores(i), :], -1e30)
            e = jnp.exp(s - jnp.max(s, axis=1, keepdims=True))
            p = (e * pl.reciprocal(jnp.sum(e, axis=1, keepdims=True))).astype(BF16)
            r["p"][unit_rows(unit, i), :] = p

        def weigh(i):
            c, j = units[i]
            v = Q[rows_of(c), pl.ds(2 * D + j * LANES, LANES)].astype(BF16)
            o = merge_heads(dot(r["p"][unit_rows(unit, i), :], v), low)
            O[rows_of(c), pl.ds(j * LANES, LANES)] = o

        if PHASES:
            for stage in (score, soften, weigh):
                staged([stage], len(units))
        else:
            staged([score, soften, weigh], len(units))
        o = O[...].astype(BF16)
        r["o"][here, :] = o
        H[...] += dot(o, r["proj_w"][...]) + r["ob"][0:1]
        for at in range(0, R, SUB):
            res = H[pl.ds(at, SUB), :]
            vh2, rs2 = norm_stats(res)
            r["rs2"][saved(at, SUB), :] = rs2
            r["vh2"][saved(at, SUB), :] = vh2.astype(BF16)
            r["n2"][saved(at, SUB), :] = (vh2 * r["gain"][1:2] + r["bias"][1:2]).astype(BF16)
            H[pl.ds(at, SUB), :] = res + r["ob"][1:2]

        def enter(i):
            j, part = divmod(i, R // HALF)
            buf = (FA, FB)[j % 2]
            n2 = r["n2"][saved(part * HALF, HALF), :]
            buf[pl.ds(part * HALF, HALF), :] = dot(n2, r["fc1_w"][:, cols(j)]) + r["fc1_b"][:, cols(j)]

        def leave(i):
            j, part = divmod(i, R // HALF)
            buf = (FA, FB)[j % 2]
            for at in range(part * HALF, (part + 1) * HALF, SUB):
                u, gu = gelu_pair(buf[pl.ds(at, SUB), :])
                r["u"][saved(at, SUB), cols(j)] = u.astype(BF16)
                r["gu"][saved(at, SUB), cols(j)] = gu.astype(BF16)

        def close(i):
            j, part = divmod(i, R // HALF)
            H[pl.ds(part * HALF, HALF), :] += dot(r["u"][saved(part * HALF, HALF), cols(j)], r["fc2_w"][cols(j), :])

        staged([enter, leave, close], chunks * R // HALF)
        y = H[...].astype(BF16)
        r["yb"][here, :] = y

        @pl.when(first)
        def _():
            r["send"][mail, :] = y

    def backward(unit, k):
        base = pl.multiple_of(unit * R, 16)
        cloud0 = unit * C
        here = pl.ds(base, R)
        mail = pl.ds(pl.multiple_of(k * R, 16), R)

        def saved(at, count):
            return pl.ds(pl.multiple_of(base + at, 16), count)

        @pl.when(role != 0)
        def _():
            X[...] = jnp.zeros(X.shape, F32)
            for c in range(C):
                X[pl.ds(c * PR, rows_in), :] = r["cot"][cloud0 + c].astype(F32)

        @pl.when(first)
        def _():
            X[...] = r["recv"][mail, :].astype(F32)

        r["dyb"][here, :] = X[...].astype(BF16)
        small[2:3, pl.ds(D, D)] += colsum(X[...])

        for at in range(0, FF, GW):
            col = pl.ds(at, GW)
            df = dot_t(r["dyb"][here, :], r["fc2_w"][col, :]) * r["gu"][here, col].astype(F32)
            small[0:1, col] += colsum(df)
            dfb = df.astype(BF16)
            r["gu"][here, col] = dfb
            part = dot_t(dfb, r["fc1_w"][:, col])
            H[...] = part if at == 0 else H[...] + part
        sums = [0.0] * 3
        for at in range(0, R, SUB):
            rows = pl.ds(at, SUB)
            dn2 = H[rows, :]
            vh2 = r["vh2"][saved(at, SUB), :].astype(F32)
            dr = X[rows, :] + norm_back(dn2, r["gain"][1:2], vh2, r["rs2"][saved(at, SUB), :])
            X[rows, :] = dr
            r["vh2"][saved(at, SUB), :] = dr.astype(BF16)
            sums = [s + colsum(v) for s, v in zip(sums, (dn2 * vh2, dn2, dr))]
        for row, at, s in zip((1, 1, 2), (D, 3 * D, 0), sums):
            small[row : row + 1, pl.ds(at, D)] += s
        G[...] = dot_t(r["vh2"][here, :], r["proj_w"][...]).astype(BF16).astype(F32)
        Q[...] = r["qkv"][here, :].astype(F32)

        def do_of(i):
            c, j = units[i]
            return stack_heads(G[rows_of(c), pl.ds(j * LANES, LANES)], low).astype(BF16)

        def score(i):
            c, j = units[i]
            v = Q[rows_of(c), pl.ds(2 * D + j * LANES, LANES)].astype(BF16)
            S[scores(i), :] = dot_t(do_of(i), v)

        def soften(i):
            p = r["p"][unit_rows(unit, i), :].astype(F32)
            dp = S[scores(i), :]
            ds = p * (dp - jnp.sum(dp * p, axis=1, keepdims=True))
            S[scores(i), :] = ds * scale

        def weigh(i):
            c, j = units[i]
            at = rows_of(c)
            q_at, k_at, v_at = (pl.ds(m * D + j * LANES, LANES) for m in range(3))
            q = stack_heads(Q[at, q_at], low).astype(BF16)
            k = Q[at, k_at].astype(BF16)
            dsb = S[scores(i), :].astype(BF16)
            dq = merge_heads(dot(dsb, k), low)
            dk = dot_c(dsb, q)
            Q[at, v_at] = dot_c(r["p"][unit_rows(unit, i), :], do_of(i))
            Q[at, q_at] = dq
            Q[at, k_at] = dk

        if PHASES:
            for stage in (score, soften, weigh):
                staged([stage], len(units))
        else:
            staged([score, soften, weigh], len(units))
        for at in range(0, 3 * D, GQ):
            col = pl.ds(at, min(GQ, 3 * D - at))
            dqkv = Q[:, col].astype(BF16)
            r["qkv"][here, col] = dqkv
            part = dot_t(dqkv, r["qkv_w"][:, col])
            H[...] = part if at == 0 else H[...] + part
        sums = [0.0] * 3
        for at in range(0, R, SUB):
            rows = pl.ds(at, SUB)
            dn1 = H[rows, :]
            vh1 = r["vh1"][saved(at, SUB), :].astype(F32)
            dh = X[rows, :] + norm_back(dn1, r["gain"][0:1], vh1, r["rs1"][saved(at, SUB), :])
            X[rows, :] = dh
            r["vh1"][saved(at, SUB), :] = dh.astype(BF16)
            sums = [s + colsum(v) for s, v in zip(sums, (dn1 * vh1, dn1, dh))]
        for row, at, s in zip((1, 1, 2), (0, 2 * D, 2 * D), sums):
            small[row : row + 1, pl.ds(at, D)] += s
        dhb = r["vh1"][here, :]

        @pl.when(role != 0)
        def _():
            r["send"][mail, :] = dhb

        O[:, :LANES] = dot_t(dhb, r["pw2"][...]) * r["gz"][here, :].astype(F32)
        for c in range(C):
            cen = centre_rows(r["centers"], cloud0 + c)
            dz = jnp.concatenate([O[rows_of(c), :LANES], jnp.zeros((LANES - PR, LANES), F32)], axis=0)
            dw = dot_f32(cen, dz)
            for i in range(4):
                small[3:4, pl.ds(i * LANES, LANES)] += dw[i : i + 1]
            dx_at = pl.ds(pl.multiple_of(base + c * PR, 8), PR)

            @pl.when(first)
            def _():
                hit = masked_rows(r["mask_idx"], cloud0 + c, PR)
                dx = X[rows_of(c), :]
                r["dx"][dx_at, :] = jnp.where(hit, 0.0, dx)
                small[2:3, pl.ds(3 * D, D)] += colsum(jnp.where(hit, dx, 0.0))

            @pl.when(role != 0)
            def _():
                r["dx"][dx_at, :] = X[rows_of(c), :]

    run(0, position)
    run(1, forward)
    run(2, backward)


def tick_units(units):
    if sum(TICK_UNITS) == units:
        return TICK_UNITS
    return (1,) * units


def tick_plan(chunks, t, units):
    none = (0, 0)

    def chunk(i):
        return chunks[i] if 0 <= i < len(chunks) else none

    half = -(-units // LAG)
    early = (t * half, min(half, units - t * half)) if t < LAG else none
    ahead = [chunk(t)]
    if t >= LAG:
        ahead = [chunk(i) for i in (2 * t - LAG, 2 * t - LAG + 1)]
    ahead = [c for c in ahead if c != none]
    ahead = (ahead[0][0], sum(c[1] for c in ahead)) if ahead else none
    return (ahead, chunk(t), chunk(t - 2 * LAG)), (early, chunk(t - LAG), chunk(t - LAG))


def tick_scratch(cfg):
    (C, _, PR, D, _) = cfg
    R = C * PR
    wide = [(R, D), (R, D), (R, 3 * D), (R, D), (R, D), (C * HEADS * PR, PR), (R, HID), (R, HID)]
    return [pltpu.VMEM(shape, F32) for shape in wide]


def vmem(x):
    return pltpu.with_memory_space_constraint(x, pltpu.VMEM)


def blocked_product(left_ref, right_ref, out_ref, at):
    height = left_ref.shape[1]
    step = min(height, 384)
    for i in range(0, height, step):
        block = dot_c(left_ref[:, pl.ds(i, step)], right_ref[...]).astype(BF16)
        for j in range(right_ref.shape[1] // LANES):
            out_ref[pl.ds(at + j * height + i, step), :] = block[:, j * LANES : (j + 1) * LANES]
    return at + height * right_ref.shape[1] // LANES


def small_rows(position, small, small_got):
    width = small.shape[1]
    mask_at = 3 * width // 4
    rows = []
    for i in range(4):
        for j in range(0, width, LANES):
            row = small[i : i + 1, j : j + LANES]
            if i == 2 and j >= mask_at:
                row = jnp.where(position[0] == 0, row, small_got[i : i + 1, j : j + LANES])
            rows.append(row)
    return jnp.concatenate(rows, axis=0).astype(BF16)


def wgrad_kernel(products, with_small, position, *refs):
    *ins, keep_ref, send_ref, full = refs
    at = 0
    for i in range(products):
        at = blocked_product(ins[2 * i], ins[2 * i + 1], full, at)
    if with_small:
        rows = small_rows(position, *ins[2 * products :])
        full[pl.ds(at, rows.shape[0]), :] = rows
        at += rows.shape[0]
    if at < full.shape[0]:
        full[pl.ds(at, full.shape[0] - at), :] = jnp.zeros((full.shape[0] - at, LANES), BF16)
    half = full.shape[0] // 2
    bit = position[2]
    keep_ref[...] = full[pl.ds(pl.multiple_of(bit * half, 16), half), :]
    send_ref[...] = full[pl.ds(pl.multiple_of((1 - bit) * half, 16), half), :]


def split_kernel(step, position, keep, got, keep_ref, send_ref):
    half = keep_ref.shape[0]
    bit = position[2 + step]
    for at, out in ((bit * half, keep_ref), ((1 - bit) * half, send_ref)):
        rows = pl.ds(pl.multiple_of(at, 16), half)
        out[...] = (keep[rows, :].astype(F32) + got[rows, :].astype(F32)).astype(BF16)


def add_kernel(keep, got, out):
    out[...] = (keep[...].astype(F32) + got[...].astype(F32)).astype(BF16)


def join_kernel(step, position, mine, got, out):
    half = mine.shape[0]
    bit = position[2 + step]
    out[pl.ds(pl.multiple_of(bit * half, 16), half), :] = mine[...]
    out[pl.ds(pl.multiple_of((1 - bit) * half, 16), half), :] = got[...]


def finish_kernel(blocks, cuts, step, position, mine, got, *refs):
    *outs, full = refs
    join_kernel(step, position, mine, got, full)
    at = 0
    for out in outs[:blocks]:
        _, rows, cols = out.shape
        for j in range(cols // LANES):
            out[0, :, pl.ds(j * LANES, LANES)] = full[pl.ds(at, rows), :].astype(F32)
            at += rows
    if cuts:
        small = full[pl.ds(at, sum(cuts)), :].astype(F32)
        at = 0
        for out, count in zip(outs[blocks:], cuts):
            width = out.shape[-1]
            for k in range(count):
                row, col = divmod(k * LANES, width)
                piece = small[at + k : at + k + 1]
                if len(out.shape) == 3:
                    out[row // out.shape[1], pl.ds(row % out.shape[1], 1), pl.ds(col, LANES)] = piece
                elif len(out.shape) == 2:
                    out[:, pl.ds(col, LANES)] = piece
                else:
                    out[pl.ds(col, LANES)] = piece.reshape(LANES)
            at += count


def call(kernel, outs, position, args, scratch=(), name=None, flops=10**6):
    whole = pl.BlockSpec(memory_space=pltpu.VMEM)
    first = [] if position is None else [position]
    return pl.pallas_call(
        kernel,
        out_shape=outs,
        in_specs=[pl.BlockSpec(memory_space=pltpu.SMEM)] * len(first) + [whole] * len(args),
        out_specs=[whole] * len(outs),
        scratch_shapes=list(scratch),
        compiler_params=pltpu.CompilerParams(vmem_limit_bytes=VMEM_LIMIT),
        cost_estimate=pl.CostEstimate(flops=max(flops, 8 * 10**8), bytes_accessed=10**5, transcendentals=0),
        name=name,
    )(*first, *[vmem(a) for a in args])


def reduce_steps(n):
    steps = [(1 << b, 1 << b) for b in range(n.bit_length() - 1)]
    if len(steps) >= 3:
        steps[1], steps[2] = (2, 4), (4, 2)
    return steps


def swap(x, masks, n):
    return lax.ppermute(x, "dp", [(i, i ^ masks[i & 1]) for i in range(n)])


def upper(me, masks):
    mask = jnp.where(me & 1, masks[1], masks[0])
    return ((me & mask) != 0).astype(jnp.int32)


def group_products(group, position, n):
    name, products, extra, shapes, small_shapes = group
    height = sum(math.prod(s) for s in shapes + small_shapes) // LANES
    height = -(-height // (8 * n)) * 8 * n
    half = pltpu.VMEM((height // 2, LANES), BF16)
    flat = [x for pair in products for x in pair] + list(extra)
    work = sum(2 * l.shape[0] * l.shape[1] * r.shape[1] for l, r in products)
    keep, send = call(
        functools.partial(wgrad_kernel, len(products), bool(extra)),
        [half, half],
        position,
        flat,
        [pltpu.VMEM((height, LANES), BF16)],
        "wgrad_" + name,
        work,
    )
    keep, position = lax.optimization_barrier((keep, position))
    return (keep, send), position


def group_sums(groups, state, position, n, aside):
    steps = reduce_steps(n)
    last = len(steps) - 1
    results = [None] * len(groups)
    total = 2 * last + 1
    for t in range(total + len(groups) - 1):
        for g, (name, _, _, shapes, small_shapes) in enumerate(groups):
            s = t - g
            if not 0 <= s < total:
                continue
            keep, send = state[g]
            if s < last:
                got = swap(send, steps[s], n)
                if s + 1 < last:
                    half = pltpu.VMEM((keep.shape[0] // 2, LANES), BF16)
                    state[g] = call(
                        functools.partial(split_kernel, s + 1), [half, half], position, [keep, got], name="split"
                    )
                else:
                    (both,) = call(add_kernel, [pltpu.VMEM(keep.shape, BF16)], None, [keep, got], name="add")
                    state[g] = (both, both)
            elif s == last:
                got = swap(send, steps[last], n)
                (both,) = call(add_kernel, [pltpu.VMEM(keep.shape, BF16)], None, [keep, got], name="add")
                if g == 0:
                    both, aside = lax.optimization_barrier((both, aside))
                state[g] = (both, both)
            else:
                step = 2 * last - s
                got = swap(send, steps[step], n)
                if step > 0:
                    out = pltpu.VMEM((2 * keep.shape[0], LANES), BF16)
                    (both,) = call(
                        functools.partial(join_kernel, step), [out], position, [keep, got], name="join"
                    )
                    state[g] = (both, both)
                else:
                    results[g] = call(
                        functools.partial(
                            finish_kernel, len(shapes), [math.prod(s) // LANES for s in small_shapes], step
                        ),
                        [jax.ShapeDtypeStruct(s, F32) for s in shapes + small_shapes],
                        position,
                        [keep, got],
                        [pltpu.VMEM((2 * keep.shape[0], LANES), BF16)],
                        "finish_" + name,
                    )
    return results, aside


def shards(
    tokens,
    mask_emb,
    mask_idx,
    centers,
    cotangent,
    ln_gain,
    ln_bias,
    qkv_w,
    proj_w,
    out_bias,
    fc1_w,
    fc1_b,
    fc2_w,
    pos_w1,
    pos_b1,
    pos_w2,
    pos_b2,
):
    M, C, rows_in, D = tokens.shape
    FF = fc1_w.shape[2]
    PR = -(-rows_in // 8) * 8
    R = C * PR
    total = M * R
    role = lax.axis_index("section")
    clouds = M * C
    base_args = [
        tokens.reshape(clouds, rows_in, D),
        mask_emb,
        mask_idx.reshape(clouds, -1),
        centers.reshape(3, clouds, -1),
        cotangent.reshape(clouds, rows_in, D),
        ln_gain[0],
        ln_bias[0],
        qkv_w[0],
        proj_w[0],
        out_bias[0],
        fc1_w[0],
        fc1_b.reshape(1, FF),
        fc2_w[0],
        pos_w1.transpose(1, 0, 2),
        pos_b1.reshape(1, -1),
        pos_w2[0],
        pos_b2.reshape(1, D),
    ]
    buf_shapes = [((total, w * LANES), dt) for _, w, dt in SAVES]
    buf_shapes += [
        ((clouds * HEADS * PR, PR), BF16),
        ((total, 1), F32),
        ((total, 1), F32),
        ((total, D), F32),
        ((8, FF), F32),
    ]
    cfg = (C, rows_in, PR, D, FF)
    whole = pl.BlockSpec(memory_space=pltpu.VMEM)
    n_dp = lax.axis_size("dp")
    me = lax.axis_index("dp")
    position = jnp.stack([role, me] + [upper(me, masks) for masks in reduce_steps(n_dp)]).astype(jnp.int32)
    chunks, at = [], 0
    for count in tick_units(M):
        chunks.append((at, count))
        at += count
    made = pl.pallas_call(
        functools.partial(alloc_kernel, len(base_args)),
        out_shape=[pltpu.VMEM(x.shape, x.dtype) for x in base_args]
        + [pltpu.VMEM(s, d) for s, d in buf_shapes + [((R, D), BF16)]],
        in_specs=[pl.BlockSpec(memory_space=pl.ANY)] * len(base_args),
        out_specs=[whole] * (len(base_args) + len(buf_shapes) + 1),
        scratch_shapes=[pltpu.SemaphoreType.DMA((len(base_args),))],
        compiler_params=pltpu.CompilerParams(vmem_limit_bytes=VMEM_LIMIT),
        name="alloc",
    )(*[pltpu.with_memory_space_constraint(x, pltpu.HBM) for x in base_args])
    base_args = [vmem(x) for x in made[: len(base_args)]]
    *bufs, blank = made[len(base_args) :]

    def tick(t, bufs, recv, send_units):
        args = [position] + base_args + [vmem(recv)] + [vmem(b) for b in bufs]
        n_in = len(args)
        outs = pl.pallas_call(
            functools.partial(tick_kernel, cfg, tick_plan(chunks, t, M)),
            out_shape=[pltpu.VMEM(s, d) for s, d in buf_shapes + [((send_units * R, D), BF16)]],
            in_specs=[pl.BlockSpec(memory_space=pltpu.SMEM)] + [whole] * (n_in - 1),
            out_specs=[whole] * (len(buf_shapes) + 1),
            scratch_shapes=tick_scratch(cfg),
            input_output_aliases={n_in - len(bufs) + i: i for i in range(len(bufs))},
            compiler_params=pltpu.CompilerParams(vmem_limit_bytes=VMEM_LIMIT),
            cost_estimate=pl.CostEstimate(flops=4 * 10**9, bytes_accessed=10**6, transcendentals=0),
            name=f"tick{t}",
        )(*args)
        return list(outs[:-1]), outs[-1]

    sections = lax.axis_size("section")
    swap_sections = [(i, sections - 1 - i) for i in range(sections)]
    sent = []
    last_tick = len(chunks) + 2 * LAG - 1
    names = [s[0] for s in SAVES] + ["p", "rs1", "rs2", "dx", "small"]
    for t in range(last_tick + 1):
        recv = lax.ppermute(sent[t - LAG], "section", swap_sections) if t >= LAG else blank
        counts = [chunks[i][1] for i in (t, t - LAG) if 0 <= i < len(chunks)]
        bufs, send = tick(t, bufs, recv, max(counts, default=1))
        sent.append(send)
    b = dict(zip(names, bufs, strict=True))

    small_got = lax.ppermute(b["small"], "section", swap_sections)
    groups = [
        ("fc2", [(b["u"], b["dyb"])], (), [(1, FF, D)], []),
        ("fc1", [(b["n2"], b["gu"])], (), [(1, D, FF)], []),
        (
            "rest",
            [(b["n1"], b["qkv"]), (b["o"], b["vh2"]), (b["pc"], b["vh1"])],
            (b["small"], small_got),
            [(1, D, 3 * D), (1, D, D), (1, LANES, D)],
            [(1, FF), (1, 2, D), (1, 2, D), (1, 2, D), (1, D), (D,), (3, 1, LANES), (1, LANES), (1, FF - 4 * LANES)],
        ),
    ]
    section_out = b["yb"].reshape(M, C, PR, D)[None, :, :, :rows_in]
    section_grad = b["dx"].reshape(M, C, PR, D)[None, :, :, :rows_in]
    halves = []
    for group in groups:
        half, position = group_products(group, position, n_dp)
        halves.append(half)
    sums, (section_out, section_grad) = group_sums(groups, halves, position, n_dp, (section_out, section_grad))
    (fc2_g,), (fc1_g,), rest = sums
    qkv_g, proj_g, pos_g, fc1_b_g, gain_g, bias_g, ob_g, pb2_g, mask_g, pw1_g, pb1_g, _ = rest
    return (
        section_out,
        section_grad,
        mask_g,
        gain_g,
        bias_g,
        qkv_g,
        proj_g,
        ob_g,
        fc1_g,
        fc1_b_g,
        fc2_g,
        pw1_g.transpose(1, 0, 2),
        pb1_g,
        pos_g,
        pb2_g,
    )


def solution(mesh):
    return jax.shard_map(
        shards,
        mesh=mesh,
        in_specs=(
            P(None, "dp", None, None),
            P(),
            P(None, "dp", None),
            P(None, None, "dp", None),
            P(None, "dp", None, None),
            P("section", None, None),
            P("section", None, None),
            P("section", None, None),
            P("section", None, None),
            P("section", None, None),
            P("section", None, None),
            P("section", None),
            P("section", None, None),
            P("section", None, None),
            P("section", None),
            P("section", None, None),
            P("section", None),
        ),
        out_specs=(
            P("section", None, "dp", None, None),
            P("section", None, "dp", None, None),
            P(),
            P("section", None, None),
            P("section", None, None),
            P("section", None, None),
            P("section", None, None),
            P("section", None, None),
            P("section", None, None),
            P("section", None),
            P("section", None, None),
            P("section", None, None),
            P("section", None),
            P("section", None, None),
            P("section", None),
        ),
        check_vma=False,
    )
```

```python
import functools
import math

import jax
import jax.numpy as jnp
from jax import lax
from jax.experimental import pallas as pl
from jax.experimental.pallas import tpu as pltpu
from jax.sharding import PartitionSpec as P

HEADS = 6
HD = 64
EPS = 1e-05
LANES = 128
MIB = 1 << 20
TICK_UNITS = (1, 1, 1, 1, 1, 1)
LAG = 2
LATE = ("cot", "fc1_w", "fc2_w")
QKV_COLS = 768
HID = 256
SUB = 288
HALF = 288
GW = 1536
GQ = 768
PHASES = True
VMEM_LIMIT = 12 * MIB

F32 = jnp.float32
BF16 = jnp.bfloat16

ERF_P = 0.375
ERF_C = (
    0.21137403,
    0.21522517,
    0.16911028,
    0.27655959,
    -0.12036233,
    0.3812622,
    -0.1331683,
)
ROOT_HALF = 0.7071067811865476
HALF_LOG2_E = -0.7213475204444817
INV_ROOT_TWO_PI = 0.3989422804014327


def gelu_pair(f):
    den = 1.0 + (ERF_P * ROOT_HALF) * jnp.abs(f)
    t = pl.reciprocal(den, approx=True)
    e = jnp.exp2((f * f) * HALF_LOG2_E)
    poly = 0.5 * ERF_C[-1]
    for c in ERF_C[-2::-1]:
        poly = poly * t + 0.5 * c
    q = e * (t * poly)
    cdf = jnp.where(f >= 0, 1.0 - q, q)
    return f * cdf, cdf + f * (INV_ROOT_TWO_PI * e)


def dot(a, b):
    return jnp.dot(a, b, preferred_element_type=F32)


def dot_t(a, b):
    return lax.dot_general(a, b, (((1,), (1,)), ((), ())), preferred_element_type=F32)


def dot_c(a, b):
    return lax.dot_general(a, b, (((0,), (0,)), ((), ())), preferred_element_type=F32)


def dot_c_f32(a, b):
    return lax.dot_general(
        a, b, (((0,), (0,)), ((), ())), preferred_element_type=F32, precision=lax.Precision.HIGHEST
    )


def dot_f32(a, b):
    return jnp.dot(a, b, preferred_element_type=F32, precision=lax.Precision.HIGHEST)


def centre_rows(centers_ref, cloud):
    patch_count = centers_ref.shape[2]
    rows = [centers_ref[i, pl.ds(cloud, 1), :] for i in range(3)]
    body = jnp.concatenate(rows, axis=0)
    body = jnp.concatenate([jnp.zeros((3, 1), F32), body], axis=1)
    body = jnp.concatenate([body, jnp.zeros((3, LANES - 1 - patch_count), F32)], axis=1)
    return jnp.concatenate([body, jnp.ones((1, LANES), F32), jnp.zeros((4, LANES), F32)], axis=0)


def masked_rows(mask_idx_ref, cloud, padded):
    ids = mask_idx_ref[pl.ds(cloud, 1), :]
    rows = lax.broadcasted_iota(jnp.int32, (padded, ids.shape[1]), 0) - 1
    return jnp.max((rows == ids).astype(F32), axis=1, keepdims=True) > 0.0


def norm_stats(v):
    width = v.shape[1]
    mean = jnp.sum(v, axis=1, keepdims=True) * (1.0 / width)
    cen = v - mean
    var = jnp.sum(cen * cen, axis=1, keepdims=True) * (1.0 / width)
    rs = lax.rsqrt(var + EPS)
    return cen * rs, rs


def norm_back(dn, gain, vhat, rs):
    width = dn.shape[1]
    dg = dn * gain
    m1 = jnp.sum(dg, axis=1, keepdims=True) * (1.0 / width)
    m2 = jnp.sum(dg * vhat, axis=1, keepdims=True) * (1.0 / width)
    return rs * (dg - m1 - vhat * m2)


def colsum(v):
    return jnp.sum(v, axis=0, keepdims=True)


def stack_heads(pair, low):
    zero = jnp.zeros_like(pair)
    return jnp.concatenate([jnp.where(low, pair, zero), jnp.where(low, zero, pair)], axis=0)


def merge_heads(stacked, low):
    n = stacked.shape[0] // 2
    return jnp.where(low, stacked[:n], stacked[n:])


SAVES = (
    ("pc", 1, BF16),
    ("gz", 1, BF16),
    ("vh1", 3, BF16),
    ("n1", 3, BF16),
    ("qkv", 9, BF16),
    ("o", 3, BF16),
    ("vh2", 3, BF16),
    ("n2", 3, BF16),
    ("u", 12, BF16),
    ("gu", 12, BF16),
    ("dyb", 3, BF16),
    ("yb", 3, BF16),
)


def alloc_kernel(count, *refs):
    sources, targets, sem = refs[:count], refs[count : 2 * count], refs[-1]
    copies = [
        pltpu.make_async_copy(source, target, sem.at[i])
        for i, (source, target) in enumerate(zip(sources, targets, strict=True))
    ]
    for copy in copies:
        copy.start()
    for ref in refs[-3:-1]:
        ref[...] = jnp.zeros(ref.shape, ref.dtype)
    for copy in copies:
        copy.wait()


def tick_kernel(cfg, plan, late, *refs):
    (C, rows_in, PR, D, FF) = cfg
    R = C * PR
    names = ["position", "tokens", "memb", "mask_idx", "centers"]
    names += ["gain", "bias", "qkv_w", "proj_w", "ob", "fc1_b", "pw1", "pb1", "pw2", "pb2"]
    names += ["recv"] + (["from_" + name for name in LATE] if late else [])
    buf_names = list(LATE) + [s[0] for s in SAVES] + ["p", "rs1", "rs2", "dx", "small"]
    names += ["old_" + b for b in buf_names]
    names += buf_names + ["send"]
    scratch_names = ["X", "H", "Q", "O", "G", "S", "FA", "FB"]
    names += scratch_names + ["sem"]
    r = dict(zip(names, refs, strict=True))
    role = r["position"][0]
    first = role == 0
    pairs = HEADS // 2
    low = lax.broadcasted_iota(jnp.int32, (PR, LANES), 1) < HD
    scale = HD**-0.5
    X, H, Q, O, G, S, FA, FB = (r[s] for s in scratch_names)
    small = r["small"]
    units = [(c, j) for c in range(C) for j in range(pairs)]
    chunks = FF // HID

    def run(which, body):
        (from0, count0), (from1, count1) = plan[0][which], plan[1][which]
        if count0 == count1 == 0:
            return
        start = jnp.where(first, from0, from1)
        count = jnp.where(first, count0, count1)

        def step(k, carry):
            body(start + k, k)
            return carry

        lax.fori_loop(0, count, step, 0)

    def rows_of(c):
        return pl.ds(c * PR, PR)

    def unit_rows(unit, i):
        return pl.ds(pl.multiple_of((unit * C * pairs + i) * 2 * PR, 16), 2 * PR)

    def scores(i):
        return pl.ds(i * 2 * PR, 2 * PR)

    def cols(j):
        return pl.ds(j * HID, HID)

    def staged(stages, count):
        for i in range(count + len(stages) - 1):
            for lag, stage in enumerate(stages):
                if 0 <= i - lag < count:
                    stage(i - lag)

    def position(unit, k):
        here = pl.ds(pl.multiple_of(unit * R, 16), R)
        w1 = jnp.concatenate([r["pw1"][i] for i in range(3)] + [r["pb1"][...], jnp.zeros((4, LANES), F32)], axis=0)
        for c in range(C):
            O[rows_of(c), :LANES] = dot_c_f32(centre_rows(r["centers"], unit * C + c), w1)[:PR]
        pc, gz = gelu_pair(O[:, :LANES])
        r["pc"][here, :] = pc.astype(BF16)
        r["gz"][here, :] = gz.astype(BF16)

    def forward(unit, k):
        base = pl.multiple_of(unit * R, 16)
        cloud0 = unit * C
        here = pl.ds(base, R)
        mail = pl.ds(pl.multiple_of(k * R, 16), R)

        def saved(at, count):
            return pl.ds(pl.multiple_of(base + at, 16), count)

        @pl.when(first)
        def _():
            X[...] = jnp.zeros(X.shape, F32)
            memb = r["memb"][...].astype(F32).reshape(1, D)
            for c in range(C):
                hit = masked_rows(r["mask_idx"], cloud0 + c, PR)[:rows_in]
                tok = r["tokens"][cloud0 + c].astype(F32)
                X[pl.ds(c * PR, rows_in), :] = jnp.where(hit, memb, tok)

        @pl.when(role != 0)
        def _():
            X[...] = r["recv"][mail, :].astype(F32)

        H[...] = X[...] + dot(r["pc"][here, :], r["pw2"][...]) + r["pb2"][...]
        for at in range(0, R, SUB):
            vh1, rs1 = norm_stats(H[pl.ds(at, SUB), :])
            r["rs1"][saved(at, SUB), :] = rs1
            r["vh1"][saved(at, SUB), :] = vh1.astype(BF16)
            r["n1"][saved(at, SUB), :] = (vh1 * r["gain"][0:1] + r["bias"][0:1]).astype(BF16)
        for at in range(0, 3 * D, QKV_COLS):
            col = pl.ds(at, min(QKV_COLS, 3 * D - at))
            qkv = dot(r["n1"][here, :], r["qkv_w"][:, col]).astype(BF16)
            r["qkv"][here, col] = qkv
            Q[:, col] = qkv.astype(F32)
        key_ok = lax.broadcasted_iota(jnp.int32, (2 * PR, PR), 1) < rows_in

        def score(i):
            c, j = units[i]
            q = Q[rows_of(c), pl.ds(j * LANES, LANES)] * scale
            k = Q[rows_of(c), pl.ds(D + j * LANES, LANES)].astype(BF16)
            S[scores(i), :] = dot_t(stack_heads(q, low).astype(BF16), k)

        def soften(i):
            s = jnp.where(key_ok, S[scores(i), :], -1e30)
            e = jnp.exp(s - jnp.max(s, axis=1, keepdims=True))
            p = (e * pl.reciprocal(jnp.sum(e, axis=1, keepdims=True))).astype(BF16)
            r["p"][unit_rows(unit, i), :] = p

        def weigh(i):
            c, j = units[i]
            v = Q[rows_of(c), pl.ds(2 * D + j * LANES, LANES)].astype(BF16)
            o = merge_heads(dot(r["p"][unit_rows(unit, i), :], v), low)
            O[rows_of(c), pl.ds(j * LANES, LANES)] = o

        if PHASES:
            for stage in (score, soften, weigh):
                staged([stage], len(units))
        else:
            staged([score, soften, weigh], len(units))
        o = O[...].astype(BF16)
        r["o"][here, :] = o
        H[...] += dot(o, r["proj_w"][...]) + r["ob"][0:1]
        for at in range(0, R, SUB):
            res = H[pl.ds(at, SUB), :]
            vh2, rs2 = norm_stats(res)
            r["rs2"][saved(at, SUB), :] = rs2
            r["vh2"][saved(at, SUB), :] = vh2.astype(BF16)
            r["n2"][saved(at, SUB), :] = (vh2 * r["gain"][1:2] + r["bias"][1:2]).astype(BF16)
            H[pl.ds(at, SUB), :] = res + r["ob"][1:2]

        def enter(i):
            j, part = divmod(i, R // HALF)
            buf = (FA, FB)[j % 2]
            n2 = r["n2"][saved(part * HALF, HALF), :]
            buf[pl.ds(part * HALF, HALF), :] = dot(n2, r["fc1_w"][:, cols(j)]) + r["fc1_b"][:, cols(j)]

        def leave(i):
            j, part = divmod(i, R // HALF)
            buf = (FA, FB)[j % 2]
            for at in range(part * HALF, (part + 1) * HALF, SUB):
                u, gu = gelu_pair(buf[pl.ds(at, SUB), :])
                r["u"][saved(at, SUB), cols(j)] = u.astype(BF16)
                r["gu"][saved(at, SUB), cols(j)] = gu.astype(BF16)

        def close(i):
            j, part = divmod(i, R // HALF)
            H[pl.ds(part * HALF, HALF), :] += dot(r["u"][saved(part * HALF, HALF), cols(j)], r["fc2_w"][cols(j), :])

        staged([enter, leave, close], chunks * R // HALF)
        y = H[...].astype(BF16)
        r["yb"][here, :] = y

        @pl.when(first)
        def _():
            r["send"][mail, :] = y

    def backward(unit, k):
        base = pl.multiple_of(unit * R, 16)
        cloud0 = unit * C
        here = pl.ds(base, R)
        mail = pl.ds(pl.multiple_of(k * R, 16), R)

        def saved(at, count):
            return pl.ds(pl.multiple_of(base + at, 16), count)

        @pl.when(role != 0)
        def _():
            X[...] = jnp.zeros(X.shape, F32)
            for c in range(C):
                X[pl.ds(c * PR, rows_in), :] = r["cot"][cloud0 + c].astype(F32)

        @pl.when(first)
        def _():
            X[...] = r["recv"][mail, :].astype(F32)

        r["dyb"][here, :] = X[...].astype(BF16)
        small[2:3, pl.ds(D, D)] += colsum(X[...])

        for at in range(0, FF, GW):
            col = pl.ds(at, GW)
            df = dot_t(r["dyb"][here, :], r["fc2_w"][col, :]) * r["gu"][here, col].astype(F32)
            small[0:1, col] += colsum(df)
            dfb = df.astype(BF16)
            r["gu"][here, col] = dfb
            part = dot_t(dfb, r["fc1_w"][:, col])
            H[...] = part if at == 0 else H[...] + part
        sums = [0.0] * 3
        for at in range(0, R, SUB):
            rows = pl.ds(at, SUB)
            dn2 = H[rows, :]
            vh2 = r["vh2"][saved(at, SUB), :].astype(F32)
            dr = X[rows, :] + norm_back(dn2, r["gain"][1:2], vh2, r["rs2"][saved(at, SUB), :])
            X[rows, :] = dr
            r["vh2"][saved(at, SUB), :] = dr.astype(BF16)
            sums = [s + colsum(v) for s, v in zip(sums, (dn2 * vh2, dn2, dr))]
        for row, at, s in zip((1, 1, 2), (D, 3 * D, 0), sums):
            small[row : row + 1, pl.ds(at, D)] += s
        G[...] = dot_t(r["vh2"][here, :], r["proj_w"][...]).astype(BF16).astype(F32)
        Q[...] = r["qkv"][here, :].astype(F32)

        def do_of(i):
            c, j = units[i]
            return stack_heads(G[rows_of(c), pl.ds(j * LANES, LANES)], low).astype(BF16)

        def score(i):
            c, j = units[i]
            v = Q[rows_of(c), pl.ds(2 * D + j * LANES, LANES)].astype(BF16)
            S[scores(i), :] = dot_t(do_of(i), v)

        def soften(i):
            p = r["p"][unit_rows(unit, i), :].astype(F32)
            dp = S[scores(i), :]
            ds = p * (dp - jnp.sum(dp * p, axis=1, keepdims=True))
            S[scores(i), :] = ds * scale

        def weigh(i):
            c, j = units[i]
            at = rows_of(c)
            q_at, k_at, v_at = (pl.ds(m * D + j * LANES, LANES) for m in range(3))
            q = stack_heads(Q[at, q_at], low).astype(BF16)
            k = Q[at, k_at].astype(BF16)
            dsb = S[scores(i), :].astype(BF16)
            dq = merge_heads(dot(dsb, k), low)
            dk = dot_c(dsb, q)
            Q[at, v_at] = dot_c(r["p"][unit_rows(unit, i), :], do_of(i))
            Q[at, q_at] = dq
            Q[at, k_at] = dk

        if PHASES:
            for stage in (score, soften, weigh):
                staged([stage], len(units))
        else:
            staged([score, soften, weigh], len(units))
        for at in range(0, 3 * D, GQ):
            col = pl.ds(at, min(GQ, 3 * D - at))
            dqkv = Q[:, col].astype(BF16)
            r["qkv"][here, col] = dqkv
            part = dot_t(dqkv, r["qkv_w"][:, col])
            H[...] = part if at == 0 else H[...] + part
        sums = [0.0] * 3
        for at in range(0, R, SUB):
            rows = pl.ds(at, SUB)
            dn1 = H[rows, :]
            vh1 = r["vh1"][saved(at, SUB), :].astype(F32)
            dh = X[rows, :] + norm_back(dn1, r["gain"][0:1], vh1, r["rs1"][saved(at, SUB), :])
            X[rows, :] = dh
            r["vh1"][saved(at, SUB), :] = dh.astype(BF16)
            sums = [s + colsum(v) for s, v in zip(sums, (dn1 * vh1, dn1, dh))]
        for row, at, s in zip((1, 1, 2), (0, 2 * D, 2 * D), sums):
            small[row : row + 1, pl.ds(at, D)] += s
        dhb = r["vh1"][here, :]

        @pl.when(role != 0)
        def _():
            r["send"][mail, :] = dhb

        O[:, :LANES] = dot_t(dhb, r["pw2"][...]) * r["gz"][here, :].astype(F32)
        for c in range(C):
            cen = centre_rows(r["centers"], cloud0 + c)
            dz = jnp.concatenate([O[rows_of(c), :LANES], jnp.zeros((LANES - PR, LANES), F32)], axis=0)
            dw = dot_f32(cen, dz)
            for i in range(4):
                small[3:4, pl.ds(i * LANES, LANES)] += dw[i : i + 1]
            dx_at = pl.ds(pl.multiple_of(base + c * PR, 8), PR)

            @pl.when(first)
            def _():
                hit = masked_rows(r["mask_idx"], cloud0 + c, PR)
                dx = X[rows_of(c), :]
                r["dx"][dx_at, :] = jnp.where(hit, 0.0, dx)
                small[2:3, pl.ds(3 * D, D)] += colsum(jnp.where(hit, dx, 0.0))

            @pl.when(role != 0)
            def _():
                r["dx"][dx_at, :] = X[rows_of(c), :]

    copies = []
    if late:
        copies = [pltpu.make_async_copy(r["from_" + name], r[name], r["sem"].at[i]) for i, name in enumerate(LATE)]
    for copy in copies:
        copy.start()
    run(0, position)
    for copy in copies:
        copy.wait()
    run(1, forward)
    run(2, backward)


def tick_units(units):
    if sum(TICK_UNITS) == units:
        return TICK_UNITS
    return (1,) * units


def tick_plan(chunks, t, units):
    none = (0, 0)

    def chunk(i):
        return chunks[i] if 0 <= i < len(chunks) else none

    half = -(-units // LAG)
    early = (t * half, min(half, units - t * half)) if t < LAG else none
    ahead = [chunk(t)]
    if t >= LAG:
        ahead = [chunk(i) for i in (2 * t - LAG, 2 * t - LAG + 1)]
    ahead = [c for c in ahead if c != none]
    ahead = (ahead[0][0], sum(c[1] for c in ahead)) if ahead else none
    return (ahead, chunk(t), chunk(t - 2 * LAG)), (early, chunk(t - LAG), chunk(t - LAG))


def tick_scratch(cfg):
    (C, _, PR, D, _) = cfg
    R = C * PR
    wide = [(R, D), (R, D), (R, 3 * D), (R, D), (R, D), (C * HEADS * PR, PR), (R, HID), (R, HID)]
    return [pltpu.VMEM(shape, F32) for shape in wide] + [pltpu.SemaphoreType.DMA((len(LATE),))]


def vmem(x):
    return pltpu.with_memory_space_constraint(x, pltpu.VMEM)


def blocked_product(left_ref, right_ref, out_ref, at):
    height = left_ref.shape[1]
    step = min(height, 384)
    for i in range(0, height, step):
        block = dot_c(left_ref[:, pl.ds(i, step)], right_ref[...]).astype(BF16)
        for j in range(right_ref.shape[1] // LANES):
            out_ref[pl.ds(at + j * height + i, step), :] = block[:, j * LANES : (j + 1) * LANES]
    return at + height * right_ref.shape[1] // LANES


def small_rows(position, small, small_got):
    width = small.shape[1]
    mask_at = 3 * width // 4
    rows = []
    for i in range(4):
        for j in range(0, width, LANES):
            row = small[i : i + 1, j : j + LANES]
            if i == 2 and j >= mask_at:
                row = jnp.where(position[0] == 0, row, small_got[i : i + 1, j : j + LANES])
            rows.append(row)
    return jnp.concatenate(rows, axis=0).astype(BF16)


def wgrad_kernel(products, with_small, position, *refs):
    *ins, keep_ref, send_ref, full = refs
    at = 0
    for i in range(products):
        at = blocked_product(ins[2 * i], ins[2 * i + 1], full, at)
    if with_small:
        rows = small_rows(position, *ins[2 * products :])
        full[pl.ds(at, rows.shape[0]), :] = rows
        at += rows.shape[0]
    if at < full.shape[0]:
        full[pl.ds(at, full.shape[0] - at), :] = jnp.zeros((full.shape[0] - at, LANES), BF16)
    half = full.shape[0] // 2
    bit = position[2]
    keep_ref[...] = full[pl.ds(pl.multiple_of(bit * half, 16), half), :]
    send_ref[...] = full[pl.ds(pl.multiple_of((1 - bit) * half, 16), half), :]


def split_kernel(step, position, keep, got, keep_ref, send_ref):
    half = keep_ref.shape[0]
    bit = position[2 + step]
    for at, out in ((bit * half, keep_ref), ((1 - bit) * half, send_ref)):
        rows = pl.ds(pl.multiple_of(at, 16), half)
        out[...] = (keep[rows, :].astype(F32) + got[rows, :].astype(F32)).astype(BF16)


def add_kernel(keep, got, out):
    out[...] = (keep[...].astype(F32) + got[...].astype(F32)).astype(BF16)


def join_kernel(step, position, mine, got, out):
    half = mine.shape[0]
    bit = position[2 + step]
    out[pl.ds(pl.multiple_of(bit * half, 16), half), :] = mine[...]
    out[pl.ds(pl.multiple_of((1 - bit) * half, 16), half), :] = got[...]


def finish_kernel(blocks, cuts, step, position, mine, got, *refs):
    *outs, full = refs
    join_kernel(step, position, mine, got, full)
    at = 0
    for out in outs[:blocks]:
        _, rows, cols = out.shape
        for j in range(cols // LANES):
            out[0, :, pl.ds(j * LANES, LANES)] = full[pl.ds(at, rows), :].astype(F32)
            at += rows
    if cuts:
        small = full[pl.ds(at, sum(cuts)), :].astype(F32)
        at = 0
        for out, count in zip(outs[blocks:], cuts):
            width = out.shape[-1]
            for k in range(count):
                row, col = divmod(k * LANES, width)
                piece = small[at + k : at + k + 1]
                if len(out.shape) == 3:
                    out[row // out.shape[1], pl.ds(row % out.shape[1], 1), pl.ds(col, LANES)] = piece
                elif len(out.shape) == 2:
                    out[:, pl.ds(col, LANES)] = piece
                else:
                    out[pl.ds(col, LANES)] = piece.reshape(LANES)
            at += count


def call(kernel, outs, position, args, scratch=(), name=None, flops=10**6):
    whole = pl.BlockSpec(memory_space=pltpu.VMEM)
    first = [] if position is None else [position]
    return pl.pallas_call(
        kernel,
        out_shape=outs,
        in_specs=[pl.BlockSpec(memory_space=pltpu.SMEM)] * len(first) + [whole] * len(args),
        out_specs=[whole] * len(outs),
        scratch_shapes=list(scratch),
        compiler_params=pltpu.CompilerParams(vmem_limit_bytes=VMEM_LIMIT),
        cost_estimate=pl.CostEstimate(flops=max(flops, 16 * 10**8), bytes_accessed=10**5, transcendentals=0),
        name=name,
    )(*first, *[vmem(a) for a in args])


def reduce_steps(n):
    steps = [(1 << b, 1 << b) for b in range(n.bit_length() - 1)]
    if len(steps) >= 3:
        steps[1], steps[2] = (2, 4), (4, 2)
    return steps


def swap(x, masks, n):
    return lax.ppermute(x, "dp", [(i, i ^ masks[i & 1]) for i in range(n)])


def upper(me, masks):
    mask = jnp.where(me & 1, masks[1], masks[0])
    return ((me & mask) != 0).astype(jnp.int32)


def group_products(group, position, n):
    name, products, extra, shapes, small_shapes = group
    height = sum(math.prod(s) for s in shapes + small_shapes) // LANES
    height = -(-height // (8 * n)) * 8 * n
    half = pltpu.VMEM((height // 2, LANES), BF16)
    flat = [x for pair in products for x in pair] + list(extra)
    work = sum(2 * l.shape[0] * l.shape[1] * r.shape[1] for l, r in products)
    keep, send = call(
        functools.partial(wgrad_kernel, len(products), bool(extra)),
        [half, half],
        position,
        flat,
        [pltpu.VMEM((height, LANES), BF16)],
        "wgrad_" + name,
        work,
    )
    keep, position = lax.optimization_barrier((keep, position))
    return (keep, send), position


def group_sums(groups, state, position, n, aside):
    steps = reduce_steps(n)
    last = len(steps) - 1
    results = [None] * len(groups)
    total = 2 * last + 1
    for t in range(total + len(groups) - 1):
        for g, (name, _, _, shapes, small_shapes) in enumerate(groups):
            s = t - g
            if not 0 <= s < total:
                continue
            keep, send = state[g]
            if s < last:
                got = swap(send, steps[s], n)
                if s + 1 < last:
                    half = pltpu.VMEM((keep.shape[0] // 2, LANES), BF16)
                    state[g] = call(
                        functools.partial(split_kernel, s + 1), [half, half], position, [keep, got], name="split"
                    )
                else:
                    (both,) = call(add_kernel, [pltpu.VMEM(keep.shape, BF16)], None, [keep, got], name="add")
                    state[g] = (both, both)
            elif s == last:
                got = swap(send, steps[last], n)
                (both,) = call(add_kernel, [pltpu.VMEM(keep.shape, BF16)], None, [keep, got], name="add")
                if g == 0:
                    both, aside = lax.optimization_barrier((both, aside))
                state[g] = (both, both)
            else:
                step = 2 * last - s
                got = swap(send, steps[step], n)
                if step > 0:
                    out = pltpu.VMEM((2 * keep.shape[0], LANES), BF16)
                    (both,) = call(
                        functools.partial(join_kernel, step), [out], position, [keep, got], name="join"
                    )
                    state[g] = (both, both)
                else:
                    results[g] = call(
                        functools.partial(
                            finish_kernel, len(shapes), [math.prod(s) // LANES for s in small_shapes], step
                        ),
                        [jax.ShapeDtypeStruct(s, F32) for s in shapes + small_shapes],
                        position,
                        [keep, got],
                        [pltpu.VMEM((2 * keep.shape[0], LANES), BF16)],
                        "finish_" + name,
                    )
    return results, aside


def shards(
    tokens,
    mask_emb,
    mask_idx,
    centers,
    cotangent,
    ln_gain,
    ln_bias,
    qkv_w,
    proj_w,
    out_bias,
    fc1_w,
    fc1_b,
    fc2_w,
    pos_w1,
    pos_b1,
    pos_w2,
    pos_b2,
):
    M, C, rows_in, D = tokens.shape
    FF = fc1_w.shape[2]
    PR = -(-rows_in // 8) * 8
    R = C * PR
    total = M * R
    role = lax.axis_index("section")
    clouds = M * C
    base_args = [
        tokens.reshape(clouds, rows_in, D),
        mask_emb,
        mask_idx.reshape(clouds, -1),
        centers.reshape(3, clouds, -1),
        ln_gain[0],
        ln_bias[0],
        qkv_w[0],
        proj_w[0],
        out_bias[0],
        fc1_b.reshape(1, FF),
        pos_w1.transpose(1, 0, 2),
        pos_b1.reshape(1, -1),
        pos_w2[0],
        pos_b2.reshape(1, D),
    ]
    late_args = [cotangent.reshape(clouds, rows_in, D), fc1_w[0], fc2_w[0]]
    buf_shapes = [(x.shape, x.dtype) for x in late_args]
    buf_shapes += [((total, w * LANES), dt) for _, w, dt in SAVES]
    buf_shapes += [
        ((clouds * HEADS * PR, PR), BF16),
        ((total, 1), F32),
        ((total, 1), F32),
        ((total, D), F32),
        ((8, FF), F32),
    ]
    cfg = (C, rows_in, PR, D, FF)
    whole = pl.BlockSpec(memory_space=pltpu.VMEM)
    n_dp = lax.axis_size("dp")
    me = lax.axis_index("dp")
    position = jnp.stack([role, me] + [upper(me, masks) for masks in reduce_steps(n_dp)]).astype(jnp.int32)
    chunks, at = [], 0
    for count in tick_units(M):
        chunks.append((at, count))
        at += count
    made = pl.pallas_call(
        functools.partial(alloc_kernel, len(base_args)),
        out_shape=[pltpu.VMEM(x.shape, x.dtype) for x in base_args]
        + [pltpu.VMEM(s, d) for s, d in buf_shapes + [((R, D), BF16)]],
        in_specs=[pl.BlockSpec(memory_space=pl.ANY)] * len(base_args),
        out_specs=[whole] * (len(base_args) + len(buf_shapes) + 1),
        scratch_shapes=[pltpu.SemaphoreType.DMA((len(base_args),))],
        compiler_params=pltpu.CompilerParams(vmem_limit_bytes=VMEM_LIMIT),
        name="alloc",
    )(*[pltpu.with_memory_space_constraint(x, pltpu.HBM) for x in base_args])
    base_args = [vmem(x) for x in made[: len(base_args)]]
    *bufs, blank = made[len(base_args) :]

    def tick(t, bufs, recv, send_units):
        late = [pltpu.with_memory_space_constraint(x, pltpu.HBM) for x in late_args] if t == 0 else []
        args = [position] + base_args + [vmem(recv)] + late + [vmem(b) for b in bufs]
        n_in = len(args)
        outs = pl.pallas_call(
            functools.partial(tick_kernel, cfg, tick_plan(chunks, t, M), t == 0),
            out_shape=[pltpu.VMEM(s, d) for s, d in buf_shapes + [((send_units * R, D), BF16)]],
            in_specs=[pl.BlockSpec(memory_space=pltpu.SMEM)]
            + [whole] * (len(base_args) + 1)
            + [pl.BlockSpec(memory_space=pl.ANY)] * len(late)
            + [whole] * len(bufs),
            out_specs=[whole] * (len(buf_shapes) + 1),
            scratch_shapes=tick_scratch(cfg),
            input_output_aliases={n_in - len(bufs) + i: i for i in range(len(bufs))},
            compiler_params=pltpu.CompilerParams(vmem_limit_bytes=VMEM_LIMIT),
            cost_estimate=pl.CostEstimate(flops=4 * 10**9, bytes_accessed=10**6, transcendentals=0),
            name=f"tick{t}",
        )(*args)
        return list(outs[:-1]), outs[-1]

    sections = lax.axis_size("section")
    swap_sections = [(i, sections - 1 - i) for i in range(sections)]
    sent = []
    last_tick = len(chunks) + 2 * LAG - 1
    names = list(LATE) + [s[0] for s in SAVES] + ["p", "rs1", "rs2", "dx", "small"]
    for t in range(last_tick + 1):
        recv = lax.ppermute(sent[t - LAG], "section", swap_sections) if t >= LAG else blank
        counts = [chunks[i][1] for i in (t, t - LAG) if 0 <= i < len(chunks)]
        bufs, send = tick(t, bufs, recv, max(counts, default=1))
        sent.append(send)
    b = dict(zip(names, bufs, strict=True))

    small_got = lax.ppermute(b["small"], "section", swap_sections)
    groups = [
        ("fc2", [(b["u"], b["dyb"])], (), [(1, FF, D)], []),
        ("fc1", [(b["n2"], b["gu"])], (), [(1, D, FF)], []),
        (
            "rest",
            [(b["n1"], b["qkv"]), (b["o"], b["vh2"]), (b["pc"], b["vh1"])],
            (b["small"], small_got),
            [(1, D, 3 * D), (1, D, D), (1, LANES, D)],
            [(1, FF), (1, 2, D), (1, 2, D), (1, 2, D), (1, D), (D,), (3, 1, LANES), (1, LANES), (1, FF - 4 * LANES)],
        ),
    ]
    section_out = b["yb"].reshape(M, C, PR, D)[None, :, :, :rows_in]
    section_grad = b["dx"].reshape(M, C, PR, D)[None, :, :, :rows_in]
    halves = []
    for group in groups:
        half, position = group_products(group, position, n_dp)
        halves.append(half)
    sums, (section_out, section_grad) = group_sums(groups, halves, position, n_dp, (section_out, section_grad))
    (fc2_g,), (fc1_g,), rest = sums
    qkv_g, proj_g, pos_g, fc1_b_g, gain_g, bias_g, ob_g, pb2_g, mask_g, pw1_g, pb1_g, _ = rest
    return (
        section_out,
        section_grad,
        mask_g,
        gain_g,
        bias_g,
        qkv_g,
        proj_g,
        ob_g,
        fc1_g,
        fc1_b_g,
        fc2_g,
        pw1_g.transpose(1, 0, 2),
        pb1_g,
        pos_g,
        pb2_g,
    )


def solution(mesh):
    return jax.shard_map(
        shards,
        mesh=mesh,
        in_specs=(
            P(None, "dp", None, None),
            P(),
            P(None, "dp", None),
            P(None, None, "dp", None),
            P(None, "dp", None, None),
            P("section", None, None),
            P("section", None, None),
            P("section", None, None),
            P("section", None, None),
            P("section", None, None),
            P("section", None, None),
            P("section", None),
            P("section", None, None),
            P("section", None, None),
            P("section", None),
            P("section", None, None),
            P("section", None),
        ),
        out_specs=(
            P("section", None, "dp", None, None),
            P("section", None, "dp", None, None),
            P(),
            P("section", None, None),
            P("section", None, None),
            P("section", None, None),
            P("section", None, None),
            P("section", None, None),
            P("section", None, None),
            P("section", None),
            P("section", None, None),
            P("section", None, None),
            P("section", None),
            P("section", None, None),
            P("section", None),
        ),
        check_vma=False,
    )
```
